512 devices in a mesh: cfg: 2 (over core), patch: 64 (over z_lo, x, y), head: 4 (over z_hi).
Axes of the slice: x: 4, y: 8, z: 8 (z_hi: 4, z_lo: 2; z = z_hi * 2 + z_lo), core: 2. Of those that a mesh axis runs over, the one named last changes fastest.
Arguments:
- queries: bfloat16 [2, 1536, 2560], P('cfg', 'patch', 'head'), may hold values from -180 to 180
- keys_new: bfloat16 [2, 1536, 2560], P('cfg', 'patch', 'head'), may hold values from -6 to 6
- values_new: bfloat16 [2, 1536, 2560], P('cfg', 'patch', 'head'), may hold values from -6 to 6
- cache_table: bfloat16 [2, 2, 256, 2560], P('cfg', None, None, 'head'), may hold values from -6 to 6
- exponents: int32 [2, 2, 192, 20], P('cfg', None, 'patch', 'head'), may hold values from -8 to -6
- patch_layout: int32 [1536], replicated, may hold values from 0 to 255
- out_weight: bfloat16 [2560, 2560], P('head'), may hold values from -0.125 to 0.125
- gate_table: float32 [50, 2560], P(None, ('cfg', 'head')), may hold values from 0.25 to 2
- timestep: int32 [1], replicated, may hold values from 0 to 49
Outputs:
- guided: bfloat16 [1536, 2560], P('patch', ('cfg', 'head'))
The draws below stay inside these ranges and needn't reach their ends.
All inputs are finite; a program needn't handle non-finite values.
Results may differ from the reference program's by a relative error of at most 0.017.
The reference program's roundings to bfloat16 on the way (of `probs` and `attended`) count: a program that leaves them out, or rounds other values in their place, can miss the bound.
Values may be sent and summed in bfloat16 or wider, within the bound.
A program may use at most 64 MiB of HBM per device.

```python
import math
import jax
import jax.numpy as jnp
import numpy as np
from jax import lax

HEADS = 20
HEAD_DIM = 128
DOUT = 2560
TOK_DEV = 24
CACHE = 256
STEPS = 50
BLOCK = 8
TOKENS = 1536
CHANNELS = 2560
N_PATCH = 64


def base_keys(key, spread):
    normal = jax.random.truncated_normal(jax.random.fold_in(key, 101), -6.0, 6.0, (2, TOKENS, CHANNELS), jnp.float32)
    positions = jnp.arange(TOKENS)
    dup_rows = (positions % 509 == 3) & (spread > 0.0)
    rolled = jnp.roll(normal, 1, axis=1)
    return jnp.where(dup_rows[None, :, None], jnp.clip(rolled, -6.0, 6.0), normal)


def draw_keys_new(key, part):
    key_draw = base_keys(key, 0.0)
    return key_draw.astype(jnp.bfloat16)


def draw_queries(key, part):
    own_key = jax.random.fold_in(key, 2)
    queries = jax.random.truncated_normal(own_key, -6.0, 6.0, (2, TOKENS, CHANNELS), jnp.float32)
    return queries.astype(jnp.bfloat16)


def set_ends(array, key, smallest, top_value):
    dims = array.shape
    spot = [jax.random.randint(jax.random.fold_in(key, axis), (), 0, dims[axis]) for axis in range(len(dims))]
    array = array.at[tuple(spot)].set(smallest)
    longest = dims.index(max(dims))
    spot[longest] = (spot[longest] + 1) % dims[longest]
    return array.at[tuple(spot)].set(top_value)


def block_levels(stream_key, extent, pieces, smallest, high):
    loudness, own = 1.0, jax.random.fold_in(stream_key, 6)
    for dim, parts in pieces:
        heights = jnp.exp(jax.random.uniform(jax.random.fold_in(own, dim), (parts,), jnp.float32, smallest / len(pieces), high / len(pieces)))
        loudness = loudness * jnp.repeat(heights, extent[dim] // parts).reshape([-1 if axis == dim else 1 for axis in range(len(extent))])
    return loudness


def normal_values(key, extent, scale, reach, split=(), held_as=jnp.bfloat16):
    level = block_levels(key, extent, split, -0.22, 0.18) if split else 1.0
    drawn = jax.random.normal(key, extent, jnp.float32) * scale * level
    return jnp.minimum(jnp.maximum(drawn, -reach), reach).astype(held_as)


def setup_inputs(seed: int = 0) -> dict:
    key_list = jax.random.split(jax.random.key(seed), 10)
    return {
        "queries": draw_queries(jax.random.fold_in(key_list[9], 71), 0),
        "keys_new": draw_keys_new(jax.random.fold_in(key_list[9], 71), 0),
        "values_new": normal_values(key_list[2], (2, TOKENS, CHANNELS), 1.0, 6.0, ((0, 2), (1, 64), (2, 4))),
        "cache_table": normal_values(key_list[3], (2, 2, CACHE, CHANNELS), 1.0, 6.0, ((0, 2), (3, 4))),
        "exponents": set_ends(jax.random.randint(key_list[4], (2, 2, TOKENS // BLOCK, HEADS), -8, -5), jax.random.fold_in(key_list[4], 1), -8, (-5) - 1).astype(jnp.int32),
        "patch_layout": set_ends(jax.random.randint(key_list[5], (TOKENS,), 0, CACHE), jax.random.fold_in(key_list[5], 1), 0, CACHE - 1).astype(jnp.int32),
        "out_weight": normal_values(key_list[6], (CHANNELS, DOUT), CHANNELS ** -0.5, 0.125, ((0, 4),)),
        "gate_table": jnp.clip(0.25 + 1.75 * jax.random.uniform(key_list[7], (STEPS, DOUT), jnp.float32) ** block_levels(key_list[7], (STEPS, DOUT), ((1, 8),), -0.2, 0.2), 0.25, 2.0),
        "timestep": jax.random.randint(key_list[8], (1,), 0, STEPS).astype(jnp.int32),
    }


def power_two(exponent):
    powers_exp = np.arange(-12, 1)
    power_table = np.power(2.0, powers_exp).astype(np.float32)
    matches = exponent[..., None] == jnp.asarray(powers_exp, jnp.int32)
    return lax.optimization_barrier(jnp.sum(jnp.where(matches, jnp.asarray(power_table, jnp.float32), jnp.float32(0.0)), axis=-1))

def expand_scale(exponent, head_dim):
    factor = power_two(exponent)
    factor = jnp.repeat(factor, BLOCK, axis=0)
    return jnp.repeat(factor, head_dim, axis=1)

def quantize(fresh_rows, cached, factor):
    difference = fresh_rows.astype(jnp.float32) - cached.astype(jnp.float32)
    scaled = jnp.clip(difference / factor, -448.0, 448.0).astype(jnp.bfloat16)
    return (scaled.astype(jnp.float32) * factor).astype(jnp.bfloat16)

def rebuild(cached, residual):
    return (cached.astype(jnp.float32) + residual.astype(jnp.float32)).astype(jnp.bfloat16)

def reference(queries, keys_new, values_new, cache_table, exponents, patch_layout, out_weight, gate_table, timestep):
    gate_row = jnp.take(gate_table, timestep, axis=0)[0]
    inverse_root = 1.0 / math.sqrt(HEAD_DIM)
    predictions = []
    for branch in range(2):
        cached_keys = jnp.take(cache_table[branch, 0], patch_layout, axis=0)
        cached_values = jnp.take(cache_table[branch, 1], patch_layout, axis=0)
        key_residual = quantize(keys_new[branch], cached_keys, expand_scale(exponents[branch, 0], HEAD_DIM))
        value_residual = quantize(values_new[branch], cached_values, expand_scale(exponents[branch, 1], HEAD_DIM))
        key_full = rebuild(cached_keys, key_residual).astype(jnp.float32).reshape(TOKENS, HEADS, HEAD_DIM)
        value_full = rebuild(cached_values, value_residual).astype(jnp.float32).reshape(TOKENS, HEADS, HEAD_DIM)
        query_blocks = queries[branch].astype(jnp.float32).reshape(N_PATCH, TOK_DEV, HEADS, HEAD_DIM)

        def attend(query_block):
            scores = jnp.einsum('qhd,khd->hqk', query_block, key_full) * inverse_root
            row_max = lax.optimization_barrier(jnp.max(scores, axis=-1, keepdims=True))
            weights = jnp.exp(scores - row_max)
            totals = lax.optimization_barrier(jnp.sum(weights, axis=-1))
            probs = weights.astype(jnp.bfloat16).astype(jnp.float32)
            mixed_values = jnp.einsum('hqk,khd->hqd', probs, value_full)
            attended_block = mixed_values / totals[..., None]
            return attended_block.transpose(1, 0, 2).reshape(TOK_DEV, CHANNELS).astype(jnp.bfloat16)
        attended = lax.map(attend, query_blocks).reshape(TOKENS, CHANNELS)
        predictions.append(gate_row * jnp.dot(attended, out_weight, preferred_element_type=jnp.float32))
    guided = predictions[1] + 5.0 * (predictions[0] - predictions[1])
    return guided.astype(jnp.bfloat16)
```

```python
import functools
import math

import jax
import jax.numpy as jnp
from jax import lax
from jax.experimental import pallas as pl
from jax.experimental.pallas import tpu as pltpu
from jax.sharding import PartitionSpec as P

MESH = pl.DeviceIdType.MESH
BLOCK = 8
LANES = 128
GRID = (2, 4, 8)

F32 = jnp.float32
BF16 = jnp.bfloat16


def dot_t(a, b):
    return lax.dot_general(a, b, (((1,), (1,)), ((), ())), preferred_element_type=F32)


def kernel(
    n_head,
    layout,
    exponents,
    timestep,
    queries,
    keys_new,
    values_new,
    cache_table,
    out_weight,
    gate_table,
    out,
    q_in,
    k_in,
    v_in,
    table,
    weight,
    gate,
    q_all,
    kv_all,
    o_send,
    o_recv,
    a_buf,
    g_send,
    g_recv,
    local_sem,
    q_ssem,
    q_rsem,
    kv_ssem,
    kv_rsem,
    o_ssem,
    o_rsem,
    a_sem,
    g_ssem,
    g_rsem,
):
    nz, nx, ny = GRID
    nxz = nz * nx
    tok, channels = q_in.shape
    heads = channels // LANES
    rows = tok * heads
    blocks = tok // BLOCK
    half = weight.shape[1]
    width = out.shape[1]

    cfg = lax.axis_index("cfg")
    patch = lax.axis_index("patch")
    head = lax.axis_index("head")
    y = lax.rem(patch, ny)
    xz = lax.div(patch, ny)
    x = lax.rem(xz, nx)
    z = lax.div(xz, nx)

    def y_partner(step):
        return (cfg, xz * ny + lax.rem(y + step + ny, ny), head)

    def xz_partner(dz, dx):
        other_z = lax.rem(z + dz, nz)
        other_x = lax.rem(x + dx + nx, nx)
        return (cfg, (other_z * nx + other_x) * ny + y, head)

    def head_partner(step):
        return (cfg, patch, lax.rem(head + step + n_head, n_head))

    other_core = (1 - cfg, patch, head)

    local = [
        pltpu.make_async_copy(cache_table, table, local_sem.at[0]),
        pltpu.make_async_copy(keys_new, k_in, local_sem.at[1]),
        pltpu.make_async_copy(values_new, v_in, local_sem.at[2]),
        pltpu.make_async_copy(queries, q_in, local_sem.at[3]),
        pltpu.make_async_copy(
            out_weight.at[:, pl.ds(pl.multiple_of(cfg * half, LANES), half)], weight, local_sem.at[4]
        ),
        pltpu.make_async_copy(gate_table, gate, local_sem.at[5]),
    ]
    for copy in local:
        copy.start()

    partners = [y_partner(s) for s in range(1, ny)]
    partners += [xz_partner(dz, dx) for dz in range(nz) for dx in range(nx) if dz or dx]
    partners += [head_partner(s) for s in range(1, n_head)]
    partners += [other_core]
    barrier = pltpu.get_barrier_semaphore()
    for partner in partners:
        pl.semaphore_signal(barrier, inc=1, device_id=partner, device_id_type=MESH)

    local[3].wait()
    own_q = q_in[...].astype(F32)
    pad = jnp.zeros((BLOCK, LANES), F32)
    q_rows = [own_q[:, h * LANES : (h + 1) * LANES] for h in range(heads)]
    q_all[0] = jnp.concatenate(q_rows + [pad], axis=0).astype(BF16)

    lane = lax.broadcasted_iota(jnp.int32, (BLOCK, table.shape[1]), 1)
    sub = lax.broadcasted_iota(jnp.int32, (BLOCK, table.shape[1]), 0)
    picks = []
    for b in range(blocks):
        wanted = jnp.zeros(lane.shape, jnp.int32)
        for i in range(BLOCK):
            wanted = jnp.where(sub == i, layout[patch * tok + b * BLOCK + i], wanted)
        picks.append(jnp.where(lane == wanted, 1.0, 0.0).astype(F32))
    onehot = jnp.concatenate(picks, axis=0).astype(BF16)

    local[0].wait()
    local[1].wait()
    local[2].wait()
    full = []
    for kind, fresh_ref in enumerate((k_in, v_in)):
        cached = jnp.dot(onehot, table[kind], preferred_element_type=F32)
        fresh = fresh_ref[...].astype(F32)
        for h in range(heads):
            for b in range(blocks):
                power = exponents[(kind * blocks + b) * heads + h]
                factor = jnp.where(power == -8, 2.0**-8, jnp.where(power == -7, 2.0**-7, 2.0**-6))
                inverse = jnp.where(power == -8, 2.0**8, jnp.where(power == -7, 2.0**7, 2.0**6))
                where = (slice(b * BLOCK, (b + 1) * BLOCK), slice(h * LANES, (h + 1) * LANES))
                old = cached[where]
                scaled = jnp.clip((fresh[where] - old) * inverse, -448.0, 448.0)
                residual = scaled.astype(BF16).astype(F32) * factor
                full.append(old + residual)
    kv_all[0] = jnp.concatenate(full, axis=0).astype(BF16)

    pl.semaphore_wait(barrier, len(partners))

    sends = []
    for dz in reversed(range(nz)):
        for dx in range(nx):
            if dz or dx:
                e = dz * nx + dx
                copy = pltpu.make_async_remote_copy(
                    src_ref=kv_all.at[0],
                    dst_ref=kv_all.at[e],
                    send_sem=kv_ssem.at[e],
                    recv_sem=kv_rsem.at[e],
                    device_id=xz_partner(dz, dx),
                    device_id_type=MESH,
                )
                copy.start()
                sends.append(copy)
    for s in range(1, ny):
        copy = pltpu.make_async_remote_copy(
            src_ref=q_all.at[0],
            dst_ref=q_all.at[s],
            send_sem=q_ssem.at[s],
            recv_sem=q_rsem.at[s],
            device_id=y_partner(s),
            device_id_type=MESH,
        )
        copy.start()
        sends.append(copy)
    for copy in sends:
        copy.wait_recv()

    inverse_root = 1.0 / math.sqrt(LANES)
    q_f = [q_all[s].astype(F32) for s in range(ny)]
    kv_f = [kv_all[e].astype(F32) for e in range(nxz)]
    outs, lses = [], []
    for h in range(heads):
        k0, v0 = h * tok, rows + h * tok
        q_h = jnp.concatenate([q[k0 : k0 + tok] for q in q_f], axis=0).astype(BF16)
        k_h = jnp.concatenate([kv[k0 : k0 + tok] for kv in kv_f], axis=0).astype(BF16)
        v_h = jnp.concatenate([kv[v0 : v0 + tok] for kv in kv_f], axis=0).astype(BF16)
        scores = dot_t(q_h, k_h) * inverse_root
        top = jnp.max(scores, axis=1, keepdims=True)
        weights = jnp.exp(scores - top)
        total = jnp.sum(weights, axis=1, keepdims=True)
        mixed = jnp.dot(weights.astype(BF16), v_h, preferred_element_type=F32)
        outs.append(mixed / total)
        lses.append(top + jnp.log(total))

    eye = lax.broadcasted_iota(jnp.int32, (rows, LANES), 0) == lax.broadcasted_iota(
        jnp.int32, (rows, LANES), 1
    )
    sub8 = lax.broadcasted_iota(jnp.int32, (BLOCK, LANES), 0)
    o_sends = []
    for s in list(range(1, ny)) + [0]:
        part = slice(s * tok, (s + 1) * tok)
        lse = jnp.concatenate([v[part] for v in lses], axis=0)
        lse = jnp.sum(jnp.where(eye, lse, 0.0), axis=0, keepdims=True)
        high = lse.astype(BF16).astype(F32)
        mid = (lse - high).astype(BF16).astype(F32)
        low = lse - high - mid
        stats = jnp.where(sub8 == 0, high, jnp.where(sub8 == 1, mid, jnp.where(sub8 == 2, low, 0.0)))
        message = jnp.concatenate([o[part] for o in outs] + [stats], axis=0).astype(BF16)
        if s == 0:
            o_recv[0] = message
        else:
            o_send[s] = message
            copy = pltpu.make_async_remote_copy(
                src_ref=o_send.at[s],
                dst_ref=o_recv.at[s],
                send_sem=o_ssem.at[s],
                recv_sem=o_rsem.at[s],
                device_id=y_partner(-s),
                device_id_type=MESH,
            )
            copy.start()
            o_sends.append(copy)
    for copy in o_sends:
        copy.wait_recv()

    o_f = [o_recv[s].astype(F32) for s in range(ny)]
    lse_rows = []
    for o in o_f:
        stats = o[rows : rows + BLOCK]
        lse_rows.append(stats[0:1] + stats[1:2] + stats[2:3])
    top = functools.reduce(jnp.maximum, lse_rows)
    shares = [jnp.exp(v - top) for v in lse_rows]
    total = functools.reduce(jnp.add, shares)
    attended = jnp.zeros((rows, LANES), F32)
    for o, share in zip(o_f, shares):
        column = jnp.sum(jnp.where(eye, share / total, 0.0), axis=1, keepdims=True)
        attended = attended + o[:rows] * column
    a_buf[0] = jnp.concatenate([attended, pad], axis=0).astype(BF16)

    a_copy = pltpu.make_async_remote_copy(
        src_ref=a_buf.at[0],
        dst_ref=a_buf.at[1],
        send_sem=a_sem.at[0],
        recv_sem=a_sem.at[1],
        device_id=other_core,
        device_id_type=MESH,
    )
    a_copy.start()
    local[4].wait()
    local[5].wait()
    a_copy.wait_recv()

    own_a = a_buf[0].astype(F32)
    other_a = a_buf[1].astype(F32)
    stacked = jnp.concatenate(
        [
            jnp.concatenate([own_a[h * tok : (h + 1) * tok], other_a[h * tok : (h + 1) * tok]], axis=0)
            for h in range(heads)
        ],
        axis=1,
    ).astype(BF16)
    projected = jnp.dot(stacked, weight[...], preferred_element_type=F32)
    own_p, other_p = projected[:tok], projected[tok:]
    first = cfg == 0
    conditional = jnp.where(first, own_p, other_p)
    unconditional = jnp.where(first, other_p, own_p)
    mixed = unconditional + 5.0 * (conditional - unconditional)
    chunks = pl.cdiv(width, LANES)
    mixed = jnp.concatenate([mixed, jnp.zeros((tok, LANES), F32)], axis=1)
    for k in range(n_head):
        first_col = k * width
        pieces = [
            mixed[:, first_col + c * LANES : first_col + (c + 1) * LANES] for c in range(chunks)
        ]
        g_send[k] = jnp.concatenate(pieces + [pad], axis=0).astype(BF16)
    g_sends = []
    for s in range(1, n_head):
        copy = pltpu.make_async_remote_copy(
            src_ref=g_send.at[lax.rem(head + s, n_head)],
            dst_ref=g_recv.at[s],
            send_sem=g_ssem.at[s],
            recv_sem=g_rsem.at[s],
            device_id=head_partner(s),
            device_id_type=MESH,
        )
        copy.start()
        g_sends.append(copy)
    summed = g_send[head].astype(F32)
    for s, copy in enumerate(g_sends):
        copy.wait_recv()
        summed = summed + g_recv[s + 1].astype(F32)
    here = lax.broadcasted_iota(jnp.int32, gate.shape, 0) == timestep[0]
    gate_row = jnp.sum(jnp.where(here, gate[...], 0.0), axis=0, keepdims=True)
    for c in range(chunks):
        lanes = min(LANES, width - c * LANES)
        cols = slice(c * LANES, c * LANES + lanes)
        part = summed[c * tok : (c + 1) * tok, :lanes] * gate_row[:, cols]
        out[:, cols] = part.astype(out.dtype)

    for copy in sends + o_sends + [a_copy] + g_sends:
        copy.wait_send()


def solution(mesh):
    n_head = mesh.shape["head"]

    def local(
        queries,
        keys_new,
        values_new,
        cache_table,
        exponents,
        patch_layout,
        out_weight,
        gate_table,
        timestep,
    ):
        nz, nx, ny = GRID
        nxz = nz * nx
        _, tok, channels = queries.shape
        heads = channels // LANES
        rows = tok * heads
        dout = out_weight.shape[1]
        width = dout // 2 // n_head
        q_rows = rows + BLOCK
        g_rows = pl.cdiv(width, LANES) * tok + BLOCK
        any_spec = pl.BlockSpec(memory_space=pl.ANY)
        smem_spec = pl.BlockSpec(memory_space=pltpu.SMEM)
        dma = pltpu.SemaphoreType.DMA
        return pl.pallas_call(
            functools.partial(kernel, n_head),
            out_shape=jax.ShapeDtypeStruct((tok, width), BF16),
            in_specs=[smem_spec] * 3 + [any_spec] * 6,
            out_specs=pl.BlockSpec(memory_space=pltpu.VMEM),
            scratch_shapes=[
                pltpu.VMEM((tok, channels), BF16),
                pltpu.VMEM((tok, channels), BF16),
                pltpu.VMEM((tok, channels), BF16),
                pltpu.VMEM(cache_table.shape[1:], BF16),
                pltpu.VMEM((channels, dout // 2), BF16),
                pltpu.VMEM(gate_table.shape, F32),
                pltpu.VMEM((ny, q_rows, LANES), BF16),
                pltpu.VMEM((nxz, 2 * rows, LANES), BF16),
                pltpu.VMEM((ny, q_rows, LANES), BF16),
                pltpu.VMEM((ny, q_rows, LANES), BF16),
                pltpu.VMEM((2, q_rows, LANES), BF16),
                pltpu.VMEM((n_head, g_rows, LANES), BF16),
                pltpu.VMEM((n_head, g_rows, LANES), BF16),
                dma((6,)),
                dma((ny,)),
                dma((ny,)),
                dma((nxz,)),
                dma((nxz,)),
                dma((ny,)),
                dma((ny,)),
                dma((2,)),
                dma((n_head,)),
                dma((n_head,)),
            ],
            compiler_params=pltpu.CompilerParams(
                collective_id=0, has_side_effects=True, vmem_limit_bytes=60 * 2**20
            ),
        )(
            patch_layout,
            exponents.reshape(-1),
            timestep,
            queries[0],
            keys_new[0],
            values_new[0],
            cache_table[0],
            out_weight,
            gate_table,
        )

    in_specs = (
        P("cfg", "patch", "head"),
        P("cfg", "patch", "head"),
        P("cfg", "patch", "head"),
        P("cfg", None, None, "head"),
        P("cfg", None, "patch", "head"),
        P(),
        P("head", None),
        P(None, ("cfg", "head")),
        P(),
    )
    out_specs = P("patch", ("cfg", "head"))
    return jax.shard_map(local, mesh=mesh, in_specs=in_specs, out_specs=out_specs, check_vma=False)
```

```python
import functools
import math

import jax
import jax.numpy as jnp
from jax import lax
from jax.experimental import pallas as pl
from jax.experimental.pallas import tpu as pltpu
from jax.sharding import PartitionSpec as P

MESH = pl.DeviceIdType.MESH
BLOCK = 8
LANES = 128
GRID = (2, 4, 8)

F32 = jnp.float32
BF16 = jnp.bfloat16


def dot_t(a, b):
    return lax.dot_general(a, b, (((1,), (1,)), ((), ())), preferred_element_type=F32)


def far_first(count):
    return sorted(range(1, count), key=lambda step: -min(step, count - step))


def padded(count):
    return -(-count // 16) * 16


def kernel(
    n_head,
    chunks,
    layout_in,
    exponents_in,
    timestep_in,
    queries,
    keys_new,
    values_new,
    cache_table,
    out_weight,
    gate_table,
    out,
    layout,
    exponents,
    timestep,
    q_in,
    k_in,
    v_in,
    table,
    weight,
    gate,
    q_all,
    kv_all,
    o_send,
    o_recv,
    a_buf,
    projected,
    g_send,
    g_recv,
    local_sem,
    q_ssem,
    q_rsem,
    kv_ssem,
    kv_rsem,
    o_ssem,
    o_rsem,
    a_ssem,
    a_rsem,
    g_ssem,
    g_rsem,
):
    nz, nx, ny = GRID
    nxz = nz * nx
    tok = q_in.shape[0]
    heads = q_in.shape[1] // LANES
    blocks = tok // BLOCK
    half = weight.shape[1]
    width = out.shape[1]

    cfg = lax.axis_index("cfg")
    patch = lax.axis_index("patch")
    head = lax.axis_index("head")
    y = lax.rem(patch, ny)
    xz = lax.div(patch, ny)
    x = lax.rem(xz, nx)
    z = lax.div(xz, nx)

    def y_partner(step):
        return (cfg, xz * ny + lax.rem(y + step + ny, ny), head)

    def xz_partner(dz, dx):
        other_z = lax.rem(z + dz, nz)
        other_x = lax.rem(x + dx, nx)
        return (cfg, (other_z * nx + other_x) * ny + y, head)

    def head_partner(step):
        return (cfg, patch, lax.rem(head + step, n_head))

    def send(src, dst, ssem, rsem, device):
        copy = pltpu.make_async_remote_copy(
            src_ref=src,
            dst_ref=dst,
            send_sem=ssem,
            recv_sem=rsem,
            device_id=device,
            device_id_type=MESH,
        )
        copy.start()
        return copy

    other_core = (1 - cfg, patch, head)
    y_steps = far_first(ny)
    xz_steps = [(1, dx) for dx in far_first(nx)] if nz > 1 else []
    xz_steps += [(0, dx) for dx in far_first(nx)]
    xz_steps += [(1, 0)] if nz > 1 else []
    head_steps = far_first(n_head)

    partners = [y_partner(s) for s in y_steps] + [xz_partner(*s) for s in xz_steps]
    partners += [head_partner(s) for s in head_steps] + [other_core]
    barrier = pltpu.get_barrier_semaphore()
    for partner in partners:
        pl.semaphore_signal(barrier, inc=1, device_id=partner, device_id_type=MESH)
    pairs = [
        (queries, q_in),
        (layout_in, layout),
        (exponents_in, exponents),
        (cache_table, table),
        (keys_new, k_in),
        (values_new, v_in),
        (timestep_in, timestep),
        (gate_table, gate),
        (out_weight.at[:, pl.ds(pl.multiple_of(cfg * half, LANES), half)], weight),
    ]
    local = [pltpu.make_async_copy(a, b, local_sem.at[i]) for i, (a, b) in enumerate(pairs)]
    for copy in local[:6]:
        copy.start()

    local[0].wait()
    own_q = q_in[...].astype(F32)
    for c, (first, last) in enumerate(chunks):
        rows = [own_q[:, h * LANES : (h + 1) * LANES] for h in range(first, last)]
        extra = q_all[c].shape[1] - (last - first) * tok
        rows += [jnp.zeros((extra, LANES), F32)] if extra else []
        q_all[c][0] = jnp.concatenate(rows, axis=0).astype(BF16)

    local[1].wait()
    lane = lax.broadcasted_iota(jnp.int32, (BLOCK, table.shape[1]), 1)
    sub = lax.broadcasted_iota(jnp.int32, (BLOCK, table.shape[1]), 0)
    picks = []
    for b in range(blocks):
        wanted = jnp.zeros(lane.shape, jnp.int32)
        for i in range(BLOCK):
            wanted = jnp.where(sub == i, layout[patch * tok + b * BLOCK + i], wanted)
        picks.append(jnp.where(lane == wanted, 1.0, 0.0).astype(F32))
    onehot = jnp.concatenate(picks, axis=0).astype(BF16)

    for copy in local[2:6]:
        copy.wait()
    full = [[], []]
    for kind, fresh_ref in enumerate((k_in, v_in)):
        cached = jnp.dot(onehot, table[kind], preferred_element_type=F32)
        fresh = fresh_ref[...].astype(F32)
        for h in range(heads):
            for b in range(blocks):
                power = exponents[b, kind, h]
                factor = jnp.where(power == -8, 2.0**-8, jnp.where(power == -7, 2.0**-7, 2.0**-6))
                inverse = jnp.where(power == -8, 2.0**8, jnp.where(power == -7, 2.0**7, 2.0**6))
                where = (slice(b * BLOCK, (b + 1) * BLOCK), slice(h * LANES, (h + 1) * LANES))
                old = cached[where]
                scaled = jnp.clip((fresh[where] - old) * inverse, -448.0, 448.0)
                residual = scaled.astype(BF16).astype(F32) * factor
                full[kind].append(old + residual)
    for c, (first, last) in enumerate(chunks):
        part = slice(first * blocks, last * blocks)
        kv_all[c][0] = jnp.concatenate(full[0][part] + full[1][part], axis=0).astype(BF16)

    pl.semaphore_wait(barrier, len(partners))

    gathers = []
    for c in range(len(chunks)):
        copies = []
        for y_step, xz_step in zip(y_steps, xz_steps):
            q, kv = q_all[c], kv_all[c]
            slot = xz_step[0] * nx + xz_step[1]
            copies += [
                send(q.at[0], q.at[y_step], q_ssem.at[c, y_step], q_rsem.at[c, y_step], y_partner(y_step)),
                send(kv.at[0], kv.at[slot], kv_ssem.at[c, slot], kv_rsem.at[c, slot], xz_partner(*xz_step)),
            ]
        gathers.append(copies)
    for copy in local[6:]:
        copy.start()

    inverse_root = 1.0 / math.sqrt(LANES)
    sub8 = lax.broadcasted_iota(jnp.int32, (BLOCK, LANES), 0)

    def diagonal(rows):
        shape = (rows, LANES)
        return lax.broadcasted_iota(jnp.int32, shape, 0) == lax.broadcasted_iota(jnp.int32, shape, 1)

    o_sends = []
    for c, (first, last) in enumerate(chunks):
        for copy in gathers[c]:
            copy.wait_recv()
        rows = (last - first) * tok
        eye = diagonal(rows)
        q_f = [q_all[c][s].astype(F32) for s in range(ny)]
        kv_f = [kv_all[c][e].astype(F32) for e in range(nxz)]
        outs, lses = [], []
        for h in range(last - first):
            k0, v0 = h * tok, rows + h * tok
            q_h = jnp.concatenate([q[k0 : k0 + tok] for q in q_f], axis=0).astype(BF16)
            k_h = jnp.concatenate([kv[k0 : k0 + tok] for kv in kv_f], axis=0).astype(BF16)
            v_h = jnp.concatenate([kv[v0 : v0 + tok] for kv in kv_f], axis=0).astype(BF16)
            scores = dot_t(q_h, k_h) * inverse_root
            top = jnp.max(scores, axis=1, keepdims=True)
            weights = jnp.exp(scores - top)
            total = jnp.sum(weights, axis=1, keepdims=True)
            mixed = jnp.dot(weights.astype(BF16), v_h, preferred_element_type=F32)
            outs.append(mixed / total)
            lses.append(top + jnp.log(total))
        copies = []
        for s in y_steps + [0]:
            part = slice(s * tok, (s + 1) * tok)
            lse = jnp.concatenate([v[part] for v in lses], axis=0)
            lse = jnp.sum(jnp.where(eye, lse, 0.0), axis=0, keepdims=True)
            high = lse.astype(BF16).astype(F32)
            mid = (lse - high).astype(BF16).astype(F32)
            low = lse - high - mid
            stats = jnp.where(sub8 == 0, high, jnp.where(sub8 == 1, mid, jnp.where(sub8 == 2, low, 0.0)))
            extra = o_recv[c].shape[1] - rows - BLOCK
            pad = [jnp.zeros((extra, LANES), F32)] if extra else []
            message = jnp.concatenate([o[part] for o in outs] + [stats] + pad, axis=0).astype(BF16)
            if s == 0:
                o_recv[c][0] = message
            else:
                o_send[c][s] = message
                copies.append(
                    send(o_send[c].at[s], o_recv[c].at[s], o_ssem.at[c, s], o_rsem.at[c, s], y_partner(-s))
                )
        o_sends.append(copies)

    for copy in local[6:]:
        copy.wait()
    a_sends = []
    for c, (first, last) in enumerate(chunks):
        for copy in o_sends[c]:
            copy.wait_recv()
        rows = (last - first) * tok
        eye = diagonal(rows)
        o_f = [o_recv[c][s].astype(F32) for s in range(ny)]
        lse_rows = []
        for o in o_f:
            lse_rows.append(o[rows : rows + 1] + o[rows + 1 : rows + 2] + o[rows + 2 : rows + 3])
        top = functools.reduce(jnp.maximum, lse_rows)
        shares = [jnp.exp(v - top) for v in lse_rows]
        total = functools.reduce(jnp.add, shares)
        attended = jnp.zeros((rows, LANES), F32)
        for o, share in zip(o_f, shares):
            column = jnp.sum(jnp.where(eye, share / total, 0.0), axis=1, keepdims=True)
            attended = attended + o[:rows] * column
        extra = a_buf[c].shape[1] - rows
        pad = [jnp.zeros((extra, LANES), F32)] if extra else []
        a_buf[c][0] = jnp.concatenate([attended] + pad, axis=0).astype(BF16)
        swap = send(a_buf[c].at[0], a_buf[c].at[1], a_ssem.at[c], a_rsem.at[c], other_core)
        a_sends.append(swap)
        swap.wait_recv()
        own_a = a_buf[c][0].astype(F32)
        other_a = a_buf[c][1].astype(F32)
        stacked = []
        for h in range(last - first):
            part = slice(h * tok, (h + 1) * tok)
            stacked.append(jnp.concatenate([own_a[part], other_a[part]], axis=0))
        product = jnp.dot(
            jnp.concatenate(stacked, axis=1).astype(BF16),
            weight[first * LANES : last * LANES, :],
            preferred_element_type=F32,
        )
        if c < len(chunks) - 1:
            projected[...] = product if c == 0 else projected[...] + product
    product = product + projected[...]
    own_p, other_p = product[:tok], product[tok:]
    conditional = jnp.where(cfg == 0, own_p, other_p)
    unconditional = jnp.where(cfg == 0, other_p, own_p)
    mixed = unconditional + 5.0 * (conditional - unconditional)

    n_cols = pl.cdiv(width, LANES)
    mixed = jnp.concatenate([mixed, jnp.zeros((tok, LANES), F32)], axis=1)
    extra = g_send.shape[1] - n_cols * tok
    pad = [jnp.zeros((extra, LANES), F32)] if extra else []
    for k in range(n_head):
        starts = [k * width + i * LANES for i in range(n_cols)]
        g_send[k] = jnp.concatenate([mixed[:, i : i + LANES] for i in starts] + pad, axis=0).astype(BF16)
    g_sends = [
        send(g_send.at[lax.rem(head + s, n_head)], g_recv.at[s], g_ssem.at[s], g_rsem.at[s], head_partner(s))
        for s in head_steps
    ]
    here = lax.broadcasted_iota(jnp.int32, gate.shape, 0) == timestep[0]
    gate_row = jnp.sum(jnp.where(here, gate[...], 0.0), axis=0, keepdims=True)
    summed = g_send[head].astype(F32)
    for s, copy in zip(head_steps, g_sends):
        copy.wait_recv()
        summed = summed + g_recv[s].astype(F32)
    for i in range(n_cols):
        lanes = min(LANES, width - i * LANES)
        cols = slice(i * LANES, i * LANES + lanes)
        part = summed[i * tok : (i + 1) * tok, :lanes] * gate_row[:, cols]
        out[:, cols] = part.astype(out.dtype)

    for copy in sum(gathers + o_sends, []) + a_sends + g_sends:
        copy.wait_send()


def solution(mesh):
    n_head = mesh.shape["head"]

    def local(
        queries,
        keys_new,
        values_new,
        cache_table,
        exponents,
        patch_layout,
        out_weight,
        gate_table,
        timestep,
    ):
        nz, nx, ny = GRID
        nxz = nz * nx
        _, tok, channels = queries.shape
        heads = channels // LANES
        dout = out_weight.shape[1]
        width = dout // 2 // n_head
        chunks = [(0, (heads + 1) // 2), ((heads + 1) // 2, heads)]
        counts = [(last - first) * tok for first, last in chunks]
        q_rows = [padded(n) for n in counts]
        o_rows = [padded(n + BLOCK) for n in counts]
        g_rows = padded(pl.cdiv(width, LANES) * tok)
        any_spec = pl.BlockSpec(memory_space=pl.ANY)
        dma = pltpu.SemaphoreType.DMA

        def per_chunk(slots, rows):
            return [pltpu.VMEM((slots, n, LANES), BF16) for n in rows]

        n_chunk = len(chunks)
        return pl.pallas_call(
            functools.partial(kernel, n_head, chunks),
            out_shape=jax.ShapeDtypeStruct((tok, width), BF16),
            in_specs=[any_spec] * 9,
            out_specs=pl.BlockSpec(memory_space=pltpu.VMEM),
            scratch_shapes=[
                pltpu.SMEM(patch_layout.shape, jnp.int32),
                pltpu.SMEM((tok // BLOCK, 2, heads), jnp.int32),
                pltpu.SMEM((1,), jnp.int32),
                pltpu.VMEM((tok, channels), BF16),
                pltpu.VMEM((tok, channels), BF16),
                pltpu.VMEM((tok, channels), BF16),
                pltpu.VMEM(cache_table.shape[1:], BF16),
                pltpu.VMEM((channels, dout // 2), BF16),
                pltpu.VMEM(gate_table.shape, F32),
                per_chunk(ny, q_rows),
                per_chunk(nxz, [2 * n for n in counts]),
                per_chunk(ny, o_rows),
                per_chunk(ny, o_rows),
                per_chunk(2, q_rows),
                pltpu.VMEM((2 * tok, dout // 2), F32),
                pltpu.VMEM((n_head, g_rows, LANES), BF16),
                pltpu.VMEM((n_head, g_rows, LANES), BF16),
                dma((9,)),
                dma((n_chunk, ny)),
                dma((n_chunk, ny)),
                dma((n_chunk, nxz)),
                dma((n_chunk, nxz)),
                dma((n_chunk, ny)),
                dma((n_chunk, ny)),
                dma((n_chunk,)),
                dma((n_chunk,)),
                dma((n_head,)),
                dma((n_head,)),
            ],
            compiler_params=pltpu.CompilerParams(
                collective_id=0, has_side_effects=True, vmem_limit_bytes=60 * 2**20
            ),
        )(
            patch_layout,
            jnp.transpose(exponents[0], (1, 0, 2)),
            timestep,
            queries[0],
            keys_new[0],
            values_new[0],
            cache_table[0],
            out_weight,
            gate_table,
        )

    in_specs = (
        P("cfg", "patch", "head"),
        P("cfg", "patch", "head"),
        P("cfg", "patch", "head"),
        P("cfg", None, None, "head"),
        P("cfg", None, "patch", "head"),
        P(),
        P("head", None),
        P(None, ("cfg", "head")),
        P(),
    )
    out_specs = P("patch", ("cfg", "head"))
    return jax.shard_map(local, mesh=mesh, in_specs=in_specs, out_specs=out_specs, check_vma=False)
```

```python
import functools
import math

import jax
import jax.numpy as jnp
from jax import lax
from jax.experimental import pallas as pl
from jax.experimental.pallas import tpu as pltpu
from jax.sharding import PartitionSpec as P

MESH = pl.DeviceIdType.MESH
BLOCK = 8
LANES = 128
GRID = (2, 4, 8)

F32 = jnp.float32
BF16 = jnp.bfloat16


def dot_t(a, b):
    return lax.dot_general(a, b, (((1,), (1,)), ((), ())), preferred_element_type=F32)


def far_first(count):
    return sorted(range(1, count), key=lambda step: -min(step, count - step))


def padded(count):
    return -(-count // 16) * 16


def kernel(
    n_head,
    chunks,
    layout_in,
    exponents_in,
    timestep_in,
    queries,
    keys_new,
    values_new,
    cache_table,
    out_weight,
    gate_table,
    out,
    layout,
    exponents,
    timestep,
    q_in,
    k_in,
    v_in,
    table,
    weight,
    gate,
    q_all,
    kv_all,
    o_send,
    o_recv,
    a_buf,
    projected,
    g_send,
    g_recv,
    local_sem,
    q_ssem,
    q_rsem,
    kv_ssem,
    kv_rsem,
    o_ssem,
    o_rsem,
    a_ssem,
    a_rsem,
    g_ssem,
    g_rsem,
):
    nz, nx, ny = GRID
    nxz = nz * nx
    tok = q_in.shape[0]
    heads = q_in.shape[1] // LANES
    blocks = tok // BLOCK
    half = weight.shape[1]
    width = out.shape[1]

    cfg = lax.axis_index("cfg")
    patch = lax.axis_index("patch")
    head = lax.axis_index("head")
    y = lax.rem(patch, ny)
    xz = lax.div(patch, ny)
    x = lax.rem(xz, nx)
    z = lax.div(xz, nx)

    def y_partner(step):
        return (cfg, xz * ny + lax.rem(y + step + ny, ny), head)

    def xz_partner(dz, dx):
        other_z = lax.rem(z + dz, nz)
        other_x = lax.rem(x + dx, nx)
        return (cfg, (other_z * nx + other_x) * ny + y, head)

    def head_partner(step):
        return (cfg, patch, lax.rem(head + step, n_head))

    def send(src, dst, ssem, rsem, device):
        copy = pltpu.make_async_remote_copy(
            src_ref=src,
            dst_ref=dst,
            send_sem=ssem,
            recv_sem=rsem,
            device_id=device,
            device_id_type=MESH,
        )
        copy.start()
        return copy

    other_core = (1 - cfg, patch, head)
    y_steps = far_first(ny)
    xz_steps = [(1, dx) for dx in far_first(nx)] if nz > 1 else []
    xz_steps += [(0, dx) for dx in far_first(nx)]
    xz_steps += [(1, 0)] if nz > 1 else []
    head_steps = far_first(n_head)

    partners = [y_partner(s) for s in y_steps] + [xz_partner(*s) for s in xz_steps]
    partners += [head_partner(s) for s in head_steps] + [other_core]
    barrier = pltpu.get_barrier_semaphore()
    for partner in partners:
        pl.semaphore_signal(barrier, inc=1, device_id=partner, device_id_type=MESH)
    pairs = [
        (queries, q_in),
        (layout_in, layout),
        (exponents_in, exponents),
        (cache_table, table),
        (keys_new, k_in),
        (values_new, v_in),
        (timestep_in, timestep),
        (gate_table, gate),
        (out_weight.at[:, pl.ds(pl.multiple_of(cfg * half, LANES), half)], weight),
    ]
    local = [pltpu.make_async_copy(a, b, local_sem.at[i]) for i, (a, b) in enumerate(pairs)]
    for copy in local[:6]:
        copy.start()

    local[0].wait()
    own_q = q_in[...].astype(F32)
    for c, (first, last) in enumerate(chunks):
        rows = [own_q[:, h * LANES : (h + 1) * LANES] for h in range(first, last)]
        extra = q_all[c].shape[1] - (last - first) * tok
        rows += [jnp.zeros((extra, LANES), F32)] if extra else []
        q_all[c][0] = jnp.concatenate(rows, axis=0).astype(BF16)

    local[1].wait()
    lane = lax.broadcasted_iota(jnp.int32, (BLOCK, table.shape[1]), 1)
    sub = lax.broadcasted_iota(jnp.int32, (BLOCK, table.shape[1]), 0)
    picks = []
    for b in range(blocks):
        wanted = jnp.zeros(lane.shape, jnp.int32)
        for i in range(BLOCK):
            wanted = jnp.where(sub == i, layout[patch * tok + b * BLOCK + i], wanted)
        picks.append(jnp.where(lane == wanted, 1.0, 0.0).astype(F32))
    onehot = jnp.concatenate(picks, axis=0).astype(BF16)

    for copy in local[2:6]:
        copy.wait()
    full = [[], []]
    for kind, fresh_ref in enumerate((k_in, v_in)):
        cached = jnp.dot(onehot, table[kind], preferred_element_type=F32)
        fresh = fresh_ref[...].astype(F32)
        for h in range(heads):
            for b in range(blocks):
                power = exponents[b, kind, h]
                factor = jnp.where(power == -8, 2.0**-8, jnp.where(power == -7, 2.0**-7, 2.0**-6))
                inverse = jnp.where(power == -8, 2.0**8, jnp.where(power == -7, 2.0**7, 2.0**6))
                where = (slice(b * BLOCK, (b + 1) * BLOCK), slice(h * LANES, (h + 1) * LANES))
                old = cached[where]
                scaled = jnp.clip((fresh[where] - old) * inverse, -448.0, 448.0)
                residual = scaled.astype(BF16).astype(F32) * factor
                full[kind].append(old + residual)
    for c, (first, last) in enumerate(chunks):
        part = slice(first * blocks, last * blocks)
        kv_all[c][0] = jnp.concatenate(full[0][part] + full[1][part], axis=0).astype(BF16)

    pl.semaphore_wait(barrier, len(partners))

    gathers = []
    for c in range(len(chunks)):
        copies = []
        for y_step, xz_step in zip(y_steps, xz_steps):
            q, kv = q_all[c], kv_all[c]
            slot = xz_step[0] * nx + xz_step[1]
            copies += [
                send(q.at[0], q.at[y_step], q_ssem.at[c, y_step], q_rsem.at[c, y_step], y_partner(y_step)),
                send(kv.at[0], kv.at[slot], kv_ssem.at[c, slot], kv_rsem.at[c, slot], xz_partner(*xz_step)),
            ]
        gathers.append(copies)
    for copy in local[6:]:
        copy.start()

    inverse_root = 1.0 / math.sqrt(LANES)
    sub8 = lax.broadcasted_iota(jnp.int32, (BLOCK, LANES), 0)

    def diagonal(rows):
        shape = (rows, LANES)
        return lax.broadcasted_iota(jnp.int32, shape, 0) == lax.broadcasted_iota(jnp.int32, shape, 1)

    o_sends = []
    for c, (first, last) in enumerate(chunks):
        for copy in gathers[c]:
            copy.wait_recv()
        rows = (last - first) * tok
        eye = diagonal(rows)
        q_f = [q_all[c][s].astype(F32) for s in range(ny)]
        kv_f = [kv_all[c][e].astype(F32) for e in range(nxz)]
        outs, lses = [], []
        for h in range(last - first):
            k0, v0 = h * tok, rows + h * tok
            q_h = jnp.concatenate([q[k0 : k0 + tok] for q in q_f], axis=0).astype(BF16)
            k_h = jnp.concatenate([kv[k0 : k0 + tok] for kv in kv_f], axis=0).astype(BF16)
            v_h = jnp.concatenate([kv[v0 : v0 + tok] for kv in kv_f], axis=0).astype(BF16)
            scores = dot_t(q_h, k_h) * inverse_root
            top = jnp.max(scores, axis=1, keepdims=True)
            weights = jnp.exp(scores - top)
            total = jnp.sum(weights, axis=1, keepdims=True)
            mixed = jnp.dot(weights.astype(BF16), v_h, preferred_element_type=F32)
            outs.append(mixed / total)
            lses.append(top + jnp.log(total))
        copies = []
        for s in y_steps + [0]:
            part = slice(s * tok, (s + 1) * tok)
            lse = jnp.concatenate([v[part] for v in lses], axis=0)
            lse = jnp.sum(jnp.where(eye, lse, 0.0), axis=0, keepdims=True)
            high = lse.astype(BF16).astype(F32)
            mid = (lse - high).astype(BF16).astype(F32)
            low = lse - high - mid
            stats = jnp.where(sub8 == 0, high, jnp.where(sub8 == 1, mid, jnp.where(sub8 == 2, low, 0.0)))
            extra = o_recv[c].shape[1] - rows - BLOCK
            pad = [jnp.zeros((extra, LANES), F32)] if extra else []
            message = jnp.concatenate([o[part] for o in outs] + [stats] + pad, axis=0).astype(BF16)
            if s == 0:
                o_recv[c][0] = message
            else:
                o_send[c][s] = message
                copies.append(
                    send(o_send[c].at[s], o_recv[c].at[s], o_ssem.at[c, s], o_rsem.at[c, s], y_partner(-s))
                )
        o_sends.append(copies)

    for copy in local[6:]:
        copy.wait()
    def project(c):
        first, last = chunks[c]
        a_sends[c].wait_recv()
        own_a = a_buf[c][0].astype(F32)
        other_a = a_buf[c][1].astype(F32)
        stacked = []
        for h in range(last - first):
            part = slice(h * tok, (h + 1) * tok)
            stacked.append(jnp.concatenate([own_a[part], other_a[part]], axis=0))
        return jnp.dot(
            jnp.concatenate(stacked, axis=1).astype(BF16),
            weight[first * LANES : last * LANES, :],
            preferred_element_type=F32,
        )

    a_sends = []
    for c, (first, last) in enumerate(chunks):
        for copy in o_sends[c]:
            copy.wait_recv()
        rows = (last - first) * tok
        eye = diagonal(rows)
        o_f = [o_recv[c][s].astype(F32) for s in range(ny)]
        lse_rows = []
        for o in o_f:
            lse_rows.append(o[rows : rows + 1] + o[rows + 1 : rows + 2] + o[rows + 2 : rows + 3])
        top = functools.reduce(jnp.maximum, lse_rows)
        shares = [jnp.exp(v - top) for v in lse_rows]
        total = functools.reduce(jnp.add, shares)
        attended = jnp.zeros((rows, LANES), F32)
        for o, share in zip(o_f, shares):
            column = jnp.sum(jnp.where(eye, share / total, 0.0), axis=1, keepdims=True)
            attended = attended + o[:rows] * column
        extra = a_buf[c].shape[1] - rows
        pad = [jnp.zeros((extra, LANES), F32)] if extra else []
        a_buf[c][0] = jnp.concatenate([attended] + pad, axis=0).astype(BF16)
        a_sends.append(send(a_buf[c].at[0], a_buf[c].at[1], a_ssem.at[c], a_rsem.at[c], other_core))
        if c > 0:
            product = project(c - 1)
            projected[...] = product if c == 1 else projected[...] + product
    product = project(len(chunks) - 1) + projected[...]
    own_p, other_p = product[:tok], product[tok:]
    conditional = jnp.where(cfg == 0, own_p, other_p)
    unconditional = jnp.where(cfg == 0, other_p, own_p)
    mixed = unconditional + 5.0 * (conditional - unconditional)

    n_cols = pl.cdiv(width, LANES)
    mixed = jnp.concatenate([mixed, jnp.zeros((tok, LANES), F32)], axis=1)
    extra = g_send.shape[1] - n_cols * tok
    pad = [jnp.zeros((extra, LANES), F32)] if extra else []
    for k in range(n_head):
        starts = [k * width + i * LANES for i in range(n_cols)]
        g_send[k] = jnp.concatenate([mixed[:, i : i + LANES] for i in starts] + pad, axis=0).astype(BF16)
    g_sends = [
        send(g_send.at[lax.rem(head + s, n_head)], g_recv.at[s], g_ssem.at[s], g_rsem.at[s], head_partner(s))
        for s in head_steps
    ]
    here = lax.broadcasted_iota(jnp.int32, gate.shape, 0) == timestep[0]
    gate_row = jnp.sum(jnp.where(here, gate[...], 0.0), axis=0, keepdims=True)
    summed = g_send[head].astype(F32)
    for s, copy in zip(head_steps, g_sends):
        copy.wait_recv()
        summed = summed + g_recv[s].astype(F32)
    for i in range(n_cols):
        lanes = min(LANES, width - i * LANES)
        cols = slice(i * LANES, i * LANES + lanes)
        part = summed[i * tok : (i + 1) * tok, :lanes] * gate_row[:, cols]
        out[:, cols] = part.astype(out.dtype)

    for copy in sum(gathers + o_sends, []) + a_sends + g_sends:
        copy.wait_send()


def solution(mesh):
    n_head = mesh.shape["head"]

    def local(
        queries,
        keys_new,
        values_new,
        cache_table,
        exponents,
        patch_layout,
        out_weight,
        gate_table,
        timestep,
    ):
        nz, nx, ny = GRID
        nxz = nz * nx
        _, tok, channels = queries.shape
        heads = channels // LANES
        dout = out_weight.shape[1]
        width = dout // 2 // n_head
        chunks = [(0, heads // 2), (heads // 2, heads)]
        counts = [(last - first) * tok for first, last in chunks]
        q_rows = [padded(n) for n in counts]
        o_rows = [padded(n + BLOCK) for n in counts]
        g_rows = padded(pl.cdiv(width, LANES) * tok)
        any_spec = pl.BlockSpec(memory_space=pl.ANY)
        dma = pltpu.SemaphoreType.DMA

        def per_chunk(slots, rows):
            return [pltpu.VMEM((slots, n, LANES), BF16) for n in rows]

        n_chunk = len(chunks)
        return pl.pallas_call(
            functools.partial(kernel, n_head, chunks),
            out_shape=pltpu.VMEM((tok, width), BF16),
            in_specs=[any_spec] * 9,
            out_specs=pl.BlockSpec(memory_space=pltpu.VMEM),
            scratch_shapes=[
                pltpu.SMEM(patch_layout.shape, jnp.int32),
                pltpu.SMEM((tok // BLOCK, 2, heads), jnp.int32),
                pltpu.SMEM((1,), jnp.int32),
                pltpu.VMEM((tok, channels), BF16),
                pltpu.VMEM((tok, channels), BF16),
                pltpu.VMEM((tok, channels), BF16),
                pltpu.VMEM(cache_table.shape[1:], BF16),
                pltpu.VMEM((channels, dout // 2), BF16),
                pltpu.VMEM(gate_table.shape, F32),
                per_chunk(ny, q_rows),
                per_chunk(nxz, [2 * n for n in counts]),
                per_chunk(ny, o_rows),
                per_chunk(ny, o_rows),
                per_chunk(2, q_rows),
                pltpu.VMEM((2 * tok, dout // 2), F32),
                pltpu.VMEM((n_head, g_rows, LANES), BF16),
                pltpu.VMEM((n_head, g_rows, LANES), BF16),
                dma((9,)),
                dma((n_chunk, ny)),
                dma((n_chunk, ny)),
                dma((n_chunk, nxz)),
                dma((n_chunk, nxz)),
                dma((n_chunk, ny)),
                dma((n_chunk, ny)),
                dma((n_chunk,)),
                dma((n_chunk,)),
                dma((n_head,)),
                dma((n_head,)),
            ],
            compiler_params=pltpu.CompilerParams(
                collective_id=0, has_side_effects=True, vmem_limit_bytes=60 * 2**20
            ),
        )(
            patch_layout,
            jnp.transpose(exponents[0], (1, 0, 2)),
            timestep,
            queries[0],
            keys_new[0],
            values_new[0],
            cache_table[0],
            out_weight,
            gate_table,
        )

    in_specs = (
        P("cfg", "patch", "head"),
        P("cfg", "patch", "head"),
        P("cfg", "patch", "head"),
        P("cfg", None, None, "head"),
        P("cfg", None, "patch", "head"),
        P(),
        P("head", None),
        P(None, ("cfg", "head")),
        P(),
    )
    out_specs = P("patch", ("cfg", "head"))
    return jax.shard_map(local, mesh=mesh, in_specs=in_specs, out_specs=out_specs, check_vma=False)
```

```python
import functools
import math

import jax
import jax.numpy as jnp
from jax import lax
from jax.experimental import pallas as pl
from jax.experimental.pallas import tpu as pltpu
from jax.sharding import PartitionSpec as P

MESH = pl.DeviceIdType.MESH
BLOCK = 8
LANES = 128
GRID = (2, 4, 8)

F32 = jnp.float32
BF16 = jnp.bfloat16


def dot_t(a, b):
    return lax.dot_general(a, b, (((1,), (1,)), ((), ())), preferred_element_type=F32)


def far_first(count):
    return sorted(range(1, count), key=lambda step: -min(step, count - step))


def padded(count):
    return -(-count // 16) * 16


def kernel(
    n_head,
    chunks,
    layout_in,
    exponents_in,
    timestep_in,
    queries,
    keys_new,
    values_new,
    cache_table,
    out_weight,
    gate_table,
    out,
    layout,
    exponents,
    timestep,
    q_in,
    k_in,
    v_in,
    table,
    weight,
    gate,
    q_all,
    kv_all,
    o_send,
    o_recv,
    projected,
    g_send,
    g_recv,
    local_sem,
    q_ssem,
    q_rsem,
    kv_ssem,
    kv_rsem,
    o_ssem,
    o_rsem,
    g_ssem,
    g_rsem,
):
    nz, nx, ny = GRID
    nxz = nz * nx
    tok = q_in.shape[0]
    heads = q_in.shape[1] // LANES
    blocks = tok // BLOCK
    width = out.shape[1]

    cfg = lax.axis_index("cfg")
    patch = lax.axis_index("patch")
    head = lax.axis_index("head")
    y = lax.rem(patch, ny)
    xz = lax.div(patch, ny)
    x = lax.rem(xz, nx)
    z = lax.div(xz, nx)

    def y_partner(step):
        return (cfg, xz * ny + lax.rem(y + step + ny, ny), head)

    def xz_partner(dz, dx):
        other_z = lax.rem(z + dz, nz)
        other_x = lax.rem(x + dx, nx)
        return (cfg, (other_z * nx + other_x) * ny + y, head)

    def feature_partner(swap, step):
        return (1 - cfg if swap else cfg, patch, lax.rem(head + step, n_head))

    def send(src, dst, ssem, rsem, device):
        copy = pltpu.make_async_remote_copy(
            src_ref=src,
            dst_ref=dst,
            send_sem=ssem,
            recv_sem=rsem,
            device_id=device,
            device_id_type=MESH,
        )
        copy.start()
        return copy

    y_steps = far_first(ny)
    xz_steps = [(1, dx) for dx in far_first(nx)] if nz > 1 else []
    xz_steps += [(0, dx) for dx in far_first(nx)]
    xz_steps += [(1, 0)] if nz > 1 else []
    feature_steps = [(swap, s) for s in far_first(n_head) for swap in (0, 1)] + [(1, 0)]

    partners = [y_partner(s) for s in y_steps] + [xz_partner(*s) for s in xz_steps]
    partners += [feature_partner(*s) for s in feature_steps]
    pairs = [
        (queries, q_in),
        (layout_in, layout),
        (exponents_in, exponents),
        (cache_table, table),
        (keys_new, k_in),
        (values_new, v_in),
        (timestep_in, timestep),
        (gate_table, gate),
        (out_weight, weight),
    ]
    local = [pltpu.make_async_copy(a, b, local_sem.at[i]) for i, (a, b) in enumerate(pairs)]
    for copy in local[:6]:
        copy.start()
    barrier = pltpu.get_barrier_semaphore()
    for partner in partners:
        pl.semaphore_signal(barrier, inc=1, device_id=partner, device_id_type=MESH)

    local[0].wait()
    own_q = q_in[...].astype(F32)
    for c, (first, last) in enumerate(chunks):
        rows = [own_q[:, h * LANES : (h + 1) * LANES] for h in range(first, last)]
        extra = q_all[c].shape[1] - (last - first) * tok
        rows += [jnp.zeros((extra, LANES), F32)] if extra else []
        q_all[c][0] = jnp.concatenate(rows, axis=0).astype(BF16)

    local[1].wait()
    lane = lax.broadcasted_iota(jnp.int32, (BLOCK, table.shape[1]), 1)
    sub = lax.broadcasted_iota(jnp.int32, (BLOCK, table.shape[1]), 0)
    picks = []
    for b in range(blocks):
        wanted = jnp.zeros(lane.shape, jnp.int32)
        for i in range(BLOCK):
            wanted = jnp.where(sub == i, layout[patch * tok + b * BLOCK + i], wanted)
        picks.append(jnp.where(lane == wanted, 1.0, 0.0).astype(F32))
    onehot = jnp.concatenate(picks, axis=0).astype(BF16)

    for copy in local[2:6]:
        copy.wait()
    full = [[], []]
    for kind, fresh_ref in enumerate((k_in, v_in)):
        cached = jnp.dot(onehot, table[kind], preferred_element_type=F32)
        fresh = fresh_ref[...].astype(F32)
        for h in range(heads):
            for b in range(blocks):
                power = exponents[b, kind, h]
                factor = jnp.where(power == -8, 2.0**-8, jnp.where(power == -7, 2.0**-7, 2.0**-6))
                inverse = jnp.where(power == -8, 2.0**8, jnp.where(power == -7, 2.0**7, 2.0**6))
                where = (slice(b * BLOCK, (b + 1) * BLOCK), slice(h * LANES, (h + 1) * LANES))
                old = cached[where]
                scaled = jnp.clip((fresh[where] - old) * inverse, -448.0, 448.0)
                residual = scaled.astype(BF16).astype(F32) * factor
                full[kind].append(old + residual)
    for c, (first, last) in enumerate(chunks):
        part = slice(first * blocks, last * blocks)
        kv_all[c][0] = jnp.concatenate(full[0][part] + full[1][part], axis=0).astype(BF16)

    pl.semaphore_wait(barrier, len(partners))

    gathers = [[] for _ in chunks]
    for c, q in enumerate(q_all):
        for s in y_steps:
            copy = send(q.at[0], q.at[s], q_ssem.at[c, s], q_rsem.at[c, s], y_partner(s))
            gathers[c].append(copy)
    for c, kv in enumerate(kv_all):
        for dz, dx in xz_steps:
            e = dz * nx + dx
            copy = send(kv.at[0], kv.at[e], kv_ssem.at[c, e], kv_rsem.at[c, e], xz_partner(dz, dx))
            gathers[c].append(copy)
    for copy in local[6:]:
        copy.start()

    inverse_root = 1.0 / math.sqrt(LANES)
    sub8 = lax.broadcasted_iota(jnp.int32, (BLOCK, LANES), 0)

    def diagonal(rows):
        shape = (rows, LANES)
        return lax.broadcasted_iota(jnp.int32, shape, 0) == lax.broadcasted_iota(jnp.int32, shape, 1)

    o_sends = []
    for c, (first, last) in enumerate(chunks):
        for copy in gathers[c]:
            copy.wait_recv()
        rows = (last - first) * tok
        eye = diagonal(rows)
        q_f = [q_all[c][s].astype(F32) for s in range(ny)]
        kv_f = [kv_all[c][e].astype(F32) for e in range(nxz)]
        outs, lses = [], []
        for h in range(last - first):
            k0, v0 = h * tok, rows + h * tok
            q_h = jnp.concatenate([q[k0 : k0 + tok] for q in q_f], axis=0).astype(BF16)
            k_h = jnp.concatenate([kv[k0 : k0 + tok] for kv in kv_f], axis=0).astype(BF16)
            v_h = jnp.concatenate([kv[v0 : v0 + tok] for kv in kv_f], axis=0).astype(BF16)
            scores = dot_t(q_h, k_h) * inverse_root
            top = jnp.max(scores, axis=1, keepdims=True)
            weights = jnp.exp(scores - top)
            total = jnp.sum(weights, axis=1, keepdims=True)
            mixed = jnp.dot(weights.astype(BF16), v_h, preferred_element_type=F32)
            outs.append(mixed / total)
            lses.append(top + jnp.log(total))
        copies = []
        for s in y_steps + [0]:
            part = slice(s * tok, (s + 1) * tok)
            lse = jnp.concatenate([v[part] for v in lses], axis=0)
            lse = jnp.sum(jnp.where(eye, lse, 0.0), axis=0, keepdims=True)
            high = lse.astype(BF16).astype(F32)
            mid = (lse - high).astype(BF16).astype(F32)
            low = lse - high - mid
            stats = jnp.where(sub8 == 0, high, jnp.where(sub8 == 1, mid, jnp.where(sub8 == 2, low, 0.0)))
            extra = o_recv[c].shape[1] - rows - BLOCK
            pad = [jnp.zeros((extra, LANES), F32)] if extra else []
            message = jnp.concatenate([o[part] for o in outs] + [stats] + pad, axis=0).astype(BF16)
            if s == 0:
                o_recv[c][0] = message
            else:
                o_send[c][s] = message
                copies.append(
                    send(o_send[c].at[s], o_recv[c].at[s], o_ssem.at[c, s], o_rsem.at[c, s], y_partner(-s))
                )
        o_sends.append(copies)

    for copy in local[6:]:
        copy.wait()
    for c, (first, last) in enumerate(chunks):
        for copy in o_sends[c]:
            copy.wait_recv()
        rows = (last - first) * tok
        eye = diagonal(rows)
        o_f = [o_recv[c][s].astype(F32) for s in range(ny)]
        lse_rows = []
        for o in o_f:
            lse_rows.append(o[rows : rows + 1] + o[rows + 1 : rows + 2] + o[rows + 2 : rows + 3])
        top = functools.reduce(jnp.maximum, lse_rows)
        shares = [jnp.exp(v - top) for v in lse_rows]
        total = functools.reduce(jnp.add, shares)
        attended = jnp.zeros((rows, LANES), F32)
        for o, share in zip(o_f, shares):
            column = jnp.sum(jnp.where(eye, share / total, 0.0), axis=1, keepdims=True)
            attended = attended + o[:rows] * column
        by_head = [attended[h * tok : (h + 1) * tok] for h in range(last - first)]
        product = jnp.dot(
            jnp.concatenate(by_head, axis=1).astype(BF16),
            weight[first * LANES : last * LANES, :],
            preferred_element_type=F32,
        )
        if c > 0:
            product = product + projected[...]
        if c < len(chunks) - 1:
            projected[...] = product

    product = product * jnp.where(cfg == 0, 5.0, -4.0)
    n_full, rest = width // LANES, width % LANES
    lane16 = lax.broadcasted_iota(jnp.int32, (2 * BLOCK, LANES), 1)
    for k in range(2 * n_head):
        first = k * width // LANES
        odd = k % 2
        tile = first if odd else first + n_full
        half = product[:, tile * LANES : (tile + 1) * LANES]
        beside = jnp.concatenate([half[2 * BLOCK :], jnp.zeros((BLOCK, LANES), F32)], axis=0)
        own_lanes = lane16 >= rest if odd else lane16 < rest
        packed = jnp.where(own_lanes, half[: 2 * BLOCK], pltpu.roll(beside, rest, 1))
        pieces = [
            product[:, (first + odd + i) * LANES : (first + odd + i + 1) * LANES] for i in range(n_full)
        ]
        g_send[k] = jnp.concatenate(pieces + [packed], axis=0).astype(BF16)
    own_block = cfg * n_head + head
    g_sends = []
    for swap, s in feature_steps:
        slot = swap * n_head + s
        block = (1 - cfg if swap else cfg) * n_head + lax.rem(head + s, n_head)
        g_sends.append(
            send(g_send.at[block], g_recv.at[slot], g_ssem.at[slot], g_rsem.at[slot], feature_partner(swap, s))
        )
    here = lax.broadcasted_iota(jnp.int32, gate.shape, 0) == timestep[0]
    gate_row = jnp.sum(jnp.where(here, gate[...], 0.0), axis=0, keepdims=True)
    summed = g_send[own_block].astype(F32)
    for (swap, s), copy in zip(feature_steps, g_sends):
        copy.wait_recv()
        summed = summed + g_recv[swap * n_head + s].astype(F32)
    whole = [summed[i * tok : (i + 1) * tok] for i in range(n_full)]
    packed = summed[n_full * tok :]
    turned = pltpu.roll(packed, rest, 1)
    low = jnp.concatenate([packed, turned[:BLOCK]], axis=0)[:, :rest]
    high = jnp.concatenate([turned, packed[:BLOCK]], axis=0)[:, :rest]
    total = jnp.where(
        lax.rem(head, 2) == 0,
        jnp.concatenate(whole + [low], axis=1),
        jnp.concatenate([high] + whole, axis=1),
    )
    out[...] = (total * gate_row).astype(out.dtype)

    for copy in sum(gathers + o_sends, []) + g_sends:
        copy.wait_send()


def solution(mesh):
    n_head = mesh.shape["head"]

    def local(
        queries,
        keys_new,
        values_new,
        cache_table,
        exponents,
        patch_layout,
        out_weight,
        gate_table,
        timestep,
    ):
        nz, nx, ny = GRID
        nxz = nz * nx
        _, tok, channels = queries.shape
        heads = channels // LANES
        dout = out_weight.shape[1]
        width = dout // 2 // n_head
        chunks = [(0, heads // 2), (heads // 2, heads)]
        counts = [(last - first) * tok for first, last in chunks]
        q_rows = [padded(n) for n in counts]
        o_rows = [padded(n + BLOCK) for n in counts]
        g_rows = width // LANES * tok + 2 * BLOCK
        any_spec = pl.BlockSpec(memory_space=pl.ANY)
        dma = pltpu.SemaphoreType.DMA

        def per_chunk(slots, rows):
            return [pltpu.VMEM((slots, n, LANES), BF16) for n in rows]

        n_chunk = len(chunks)
        return pl.pallas_call(
            functools.partial(kernel, n_head, chunks),
            out_shape=pltpu.VMEM((tok, width), BF16),
            in_specs=[any_spec] * 9,
            out_specs=pl.BlockSpec(memory_space=pltpu.VMEM),
            scratch_shapes=[
                pltpu.SMEM(patch_layout.shape, jnp.int32),
                pltpu.SMEM((tok // BLOCK, 2, heads), jnp.int32),
                pltpu.SMEM((1,), jnp.int32),
                pltpu.VMEM((tok, channels), BF16),
                pltpu.VMEM((tok, channels), BF16),
                pltpu.VMEM((tok, channels), BF16),
                pltpu.VMEM(cache_table.shape[1:], BF16),
                pltpu.VMEM((channels, dout), BF16),
                pltpu.VMEM(gate_table.shape, F32),
                per_chunk(ny, q_rows),
                per_chunk(nxz, [2 * n for n in counts]),
                per_chunk(ny, o_rows),
                per_chunk(ny, o_rows),
                pltpu.VMEM((tok, dout), F32),
                pltpu.VMEM((2 * n_head, g_rows, LANES), BF16),
                pltpu.VMEM((2 * n_head, g_rows, LANES), BF16),
                dma((9,)),
                dma((n_chunk, ny)),
                dma((n_chunk, ny)),
                dma((n_chunk, nxz)),
                dma((n_chunk, nxz)),
                dma((n_chunk, ny)),
                dma((n_chunk, ny)),
                dma((2 * n_head,)),
                dma((2 * n_head,)),
            ],
            compiler_params=pltpu.CompilerParams(
                collective_id=0, has_side_effects=True, vmem_limit_bytes=60 * 2**20
            ),
        )(
            patch_layout,
            jnp.transpose(exponents[0], (1, 0, 2)),
            timestep,
            queries[0],
            keys_new[0],
            values_new[0],
            cache_table[0],
            out_weight,
            gate_table,
        )

    in_specs = (
        P("cfg", "patch", "head"),
        P("cfg", "patch", "head"),
        P("cfg", "patch", "head"),
        P("cfg", None, None, "head"),
        P("cfg", None, "patch", "head"),
        P(),
        P("head", None),
        P(None, ("cfg", "head")),
        P(),
    )
    out_specs = P("patch", ("cfg", "head"))
    return jax.shard_map(local, mesh=mesh, in_specs=in_specs, out_specs=out_specs, check_vma=False)
```

```python
import functools
import math

import jax
import jax.numpy as jnp
from jax import lax
from jax.experimental import pallas as pl
from jax.experimental.pallas import tpu as pltpu
from jax.sharding import PartitionSpec as P

MESH = pl.DeviceIdType.MESH
BLOCK = 8
LANES = 128
GRID = (2, 4, 8)

F32 = jnp.float32
BF16 = jnp.bfloat16


def dot_t(a, b):
    return lax.dot_general(a, b, (((1,), (1,)), ((), ())), preferred_element_type=F32)


def far_first(count):
    return sorted(range(1, count), key=lambda step: -min(step, count - step))


def padded(count):
    return -(-count // 16) * 16


def kernel(
    n_head,
    chunks,
    layout_in,
    exponents_in,
    timestep_in,
    queries,
    keys_new,
    values_new,
    cache_table,
    out_weight,
    gate_table,
    out,
    layout,
    exponents,
    timestep,
    q_in,
    k_in,
    v_in,
    table,
    weight,
    gate,
    q_all,
    kv_all,
    o_send,
    o_recv,
    projected,
    g_send,
    g_recv,
    local_sem,
    q_ssem,
    q_rsem,
    kv_ssem,
    kv_rsem,
    o_ssem,
    o_rsem,
    g_ssem,
    g_rsem,
):
    nz, nx, ny = GRID
    nxz = nz * nx
    tok = q_in.shape[0]
    heads = q_in.shape[1] // LANES
    blocks = tok // BLOCK
    width = out.shape[1]

    cfg = lax.axis_index("cfg")
    patch = lax.axis_index("patch")
    head = lax.axis_index("head")
    y = lax.rem(patch, ny)
    xz = lax.div(patch, ny)
    x = lax.rem(xz, nx)
    z = lax.div(xz, nx)

    def y_partner(step):
        return (cfg, xz * ny + lax.rem(y + step + ny, ny), head)

    def xz_partner(dz, dx):
        other_z = lax.rem(z + dz, nz)
        other_x = lax.rem(x + dx, nx)
        return (cfg, (other_z * nx + other_x) * ny + y, head)

    def feature_partner(swap, step):
        return (1 - cfg if swap else cfg, patch, lax.rem(head + step, n_head))

    def send(src, dst, ssem, rsem, device):
        copy = pltpu.make_async_remote_copy(
            src_ref=src,
            dst_ref=dst,
            send_sem=ssem,
            recv_sem=rsem,
            device_id=device,
            device_id_type=MESH,
        )
        copy.start()
        return copy

    y_steps = far_first(ny)
    xz_steps = [(1, dx) for dx in far_first(nx)] if nz > 1 else []
    xz_steps += [(0, dx) for dx in far_first(nx)]
    xz_steps += [(1, 0)] if nz > 1 else []
    feature_steps = [(swap, s) for s in far_first(n_head) for swap in (1, 0)] + [(1, 0)]

    partners = [y_partner(s) for s in y_steps] + [xz_partner(*s) for s in xz_steps]
    partners += [feature_partner(*s) for s in feature_steps]
    pairs = [
        (queries, q_in),
        (layout_in, layout),
        (exponents_in, exponents),
        (cache_table, table),
        (keys_new, k_in),
        (values_new, v_in),
        (timestep_in, timestep),
        (gate_table, gate),
        (out_weight, weight),
    ]
    local = [pltpu.make_async_copy(a, b, local_sem.at[i]) for i, (a, b) in enumerate(pairs)]
    for copy in local[:6]:
        copy.start()
    barrier = pltpu.get_barrier_semaphore()
    for partner in partners:
        pl.semaphore_signal(barrier, inc=1, device_id=partner, device_id_type=MESH)

    local[0].wait()
    own_q = q_in[...].astype(F32)
    for c, (first, last) in enumerate(chunks):
        rows = [own_q[:, h * LANES : (h + 1) * LANES] for h in range(first, last)]
        extra = q_all[c].shape[1] - (last - first) * tok
        rows += [jnp.zeros((extra, LANES), F32)] if extra else []
        q_all[c][0] = jnp.concatenate(rows, axis=0).astype(BF16)

    local[1].wait()
    lane = lax.broadcasted_iota(jnp.int32, (BLOCK, table.shape[1]), 1)
    sub = lax.broadcasted_iota(jnp.int32, (BLOCK, table.shape[1]), 0)
    picks = []
    for b in range(blocks):
        wanted = jnp.zeros(lane.shape, jnp.int32)
        for i in range(BLOCK):
            wanted = jnp.where(sub == i, layout[patch * tok + b * BLOCK + i], wanted)
        picks.append(jnp.where(lane == wanted, 1.0, 0.0).astype(F32))
    onehot = jnp.concatenate(picks, axis=0).astype(BF16)

    for copy in local[2:6]:
        copy.wait()
    full = [[], []]
    for kind, fresh_ref in enumerate((k_in, v_in)):
        cached = jnp.dot(onehot, table[kind], preferred_element_type=F32)
        fresh = fresh_ref[...].astype(F32)
        for h in range(heads):
            for b in range(blocks):
                power = exponents[b, kind, h]
                factor = jnp.where(power == -8, 2.0**-8, jnp.where(power == -7, 2.0**-7, 2.0**-6))
                inverse = jnp.where(power == -8, 2.0**8, jnp.where(power == -7, 2.0**7, 2.0**6))
                where = (slice(b * BLOCK, (b + 1) * BLOCK), slice(h * LANES, (h + 1) * LANES))
                old = cached[where]
                scaled = jnp.clip((fresh[where] - old) * inverse, -448.0, 448.0)
                residual = scaled.astype(BF16).astype(F32) * factor
                full[kind].append(old + residual)
    for c, (first, last) in enumerate(chunks):
        part = slice(first * blocks, last * blocks)
        kv_all[c][0] = jnp.concatenate(full[0][part] + full[1][part], axis=0).astype(BF16)

    pl.semaphore_wait(barrier, len(partners))

    gathers = [[] for _ in chunks]
    for c, q in enumerate(q_all):
        for s in y_steps:
            copy = send(q.at[0], q.at[s], q_ssem.at[c, s], q_rsem.at[c, s], y_partner(s))
            gathers[c].append(copy)
    for c, kv in enumerate(kv_all):
        for dz, dx in xz_steps:
            e = dz * nx + dx
            copy = send(kv.at[0], kv.at[e], kv_ssem.at[c, e], kv_rsem.at[c, e], xz_partner(dz, dx))
            gathers[c].append(copy)
    for copy in local[6:]:
        copy.start()

    inverse_root = 1.0 / math.sqrt(LANES)
    sub8 = lax.broadcasted_iota(jnp.int32, (BLOCK, LANES), 0)

    def diagonal(rows):
        shape = (rows, LANES)
        return lax.broadcasted_iota(jnp.int32, shape, 0) == lax.broadcasted_iota(jnp.int32, shape, 1)

    o_sends = []
    for c, (first, last) in enumerate(chunks):
        for copy in gathers[c]:
            copy.wait_recv()
        rows = (last - first) * tok
        eye = diagonal(rows)
        q_f = [q_all[c][s].astype(F32) for s in range(ny)]
        kv_f = [kv_all[c][e].astype(F32) for e in range(nxz)]
        outs, lses = [], []
        for h in range(last - first):
            k0, v0 = h * tok, rows + h * tok
            q_h = jnp.concatenate([q[k0 : k0 + tok] for q in q_f], axis=0).astype(BF16)
            k_h = jnp.concatenate([kv[k0 : k0 + tok] for kv in kv_f], axis=0).astype(BF16)
            v_h = jnp.concatenate([kv[v0 : v0 + tok] for kv in kv_f], axis=0).astype(BF16)
            scores = dot_t(q_h, k_h) * inverse_root
            top = jnp.max(scores, axis=1, keepdims=True)
            weights = jnp.exp(scores - top)
            total = jnp.sum(weights, axis=1, keepdims=True)
            mixed = jnp.dot(weights.astype(BF16), v_h, preferred_element_type=F32)
            outs.append(mixed / total)
            lses.append(top + jnp.log(total))
        copies = []
        for s in y_steps + [0]:
            part = slice(s * tok, (s + 1) * tok)
            lse = jnp.concatenate([v[part] for v in lses], axis=0)
            lse = jnp.sum(jnp.where(eye, lse, 0.0), axis=0, keepdims=True)
            high = lse.astype(BF16).astype(F32)
            mid = (lse - high).astype(BF16).astype(F32)
            low = lse - high - mid
            stats = jnp.where(sub8 == 0, high, jnp.where(sub8 == 1, mid, jnp.where(sub8 == 2, low, 0.0)))
            extra = o_recv[c].shape[1] - rows - BLOCK
            pad = [jnp.zeros((extra, LANES), F32)] if extra else []
            message = jnp.concatenate([o[part] for o in outs] + [stats] + pad, axis=0).astype(BF16)
            if s == 0:
                o_recv[c][0] = message
            else:
                o_send[c][s] = message
                copies.append(
                    send(o_send[c].at[s], o_recv[c].at[s], o_ssem.at[c, s], o_rsem.at[c, s], y_partner(-s))
                )
        o_sends.append(copies)

    for copy in local[6:]:
        copy.wait()
    for c, (first, last) in enumerate(chunks):
        for copy in o_sends[c]:
            copy.wait_recv()
        rows = (last - first) * tok
        eye = diagonal(rows)
        o_f = [o_recv[c][s].astype(F32) for s in range(ny)]
        lse_rows = []
        for o in o_f:
            lse_rows.append(o[rows : rows + 1] + o[rows + 1 : rows + 2] + o[rows + 2 : rows + 3])
        top = functools.reduce(jnp.maximum, lse_rows)
        shares = [jnp.exp(v - top) for v in lse_rows]
        total = functools.reduce(jnp.add, shares)
        attended = jnp.zeros((rows, LANES), F32)
        for o, share in zip(o_f, shares):
            column = jnp.sum(jnp.where(eye, share / total, 0.0), axis=1, keepdims=True)
            attended = attended + o[:rows] * column
        by_head = [attended[h * tok : (h + 1) * tok] for h in range(last - first)]
        product = jnp.dot(
            jnp.concatenate(by_head, axis=1).astype(BF16),
            weight[first * LANES : last * LANES, :],
            preferred_element_type=F32,
        )
        projected[...] = product if c == 0 else projected[...] + product

    coefficient = jnp.where(cfg == 0, 5.0, -4.0)
    n_full, rest = width // LANES, width % LANES
    lane16 = lax.broadcasted_iota(jnp.int32, (2 * BLOCK, LANES), 1)

    def features(swap, step):
        block = (1 - cfg if swap else cfg) * n_head + lax.rem(head + step, n_head)
        odd = lax.rem(block, 2) == 1
        start = pl.multiple_of(block * width // LANES * LANES, LANES)
        term = projected[:, pl.ds(start, (n_full + 1) * LANES)] * coefficient
        tiles = [term[:, i * LANES : (i + 1) * LANES] for i in range(n_full + 1)]
        half = jnp.where(odd, tiles[0], tiles[-1])
        beside = jnp.concatenate([half[2 * BLOCK :], jnp.zeros((BLOCK, LANES), F32)], axis=0)
        own_lanes = (lane16 >= rest) == odd
        packed = jnp.where(own_lanes, half[: 2 * BLOCK], pltpu.roll(beside, rest, 1))
        pieces = [jnp.where(odd, tiles[i + 1], tiles[i]) for i in range(n_full)]
        return jnp.concatenate(pieces + [packed], axis=0)

    g_sends = []
    for swap, s in feature_steps:
        slot = swap * n_head + s
        g_send[slot] = features(swap, s).astype(BF16)
        g_sends.append(
            send(g_send.at[slot], g_recv.at[slot], g_ssem.at[slot], g_rsem.at[slot], feature_partner(swap, s))
        )
    here = lax.broadcasted_iota(jnp.int32, gate.shape, 0) == timestep[0]
    gate_row = jnp.sum(jnp.where(here, gate[...], 0.0), axis=0, keepdims=True)
    summed = features(0, 0)
    for (swap, s), copy in zip(feature_steps, g_sends):
        copy.wait_recv()
        summed = summed + g_recv[swap * n_head + s].astype(F32)
    whole = [summed[i * tok : (i + 1) * tok] for i in range(n_full)]
    packed = summed[n_full * tok :]
    turned = pltpu.roll(packed, rest, 1)
    low = jnp.concatenate([packed, turned[:BLOCK]], axis=0)[:, :rest]
    high = jnp.concatenate([turned, packed[:BLOCK]], axis=0)[:, :rest]
    total = jnp.where(
        lax.rem(head, 2) == 0,
        jnp.concatenate(whole + [low], axis=1),
        jnp.concatenate([high] + whole, axis=1),
    )
    out[...] = (total * gate_row).astype(out.dtype)

    for copy in sum(gathers + o_sends, []) + g_sends:
        copy.wait_send()


def solution(mesh):
    n_head = mesh.shape["head"]

    def local(
        queries,
        keys_new,
        values_new,
        cache_table,
        exponents,
        patch_layout,
        out_weight,
        gate_table,
        timestep,
    ):
        nz, nx, ny = GRID
        nxz = nz * nx
        _, tok, channels = queries.shape
        heads = channels // LANES
        dout = out_weight.shape[1]
        width = dout // 2 // n_head
        chunks = [(0, heads // 2), (heads // 2, heads)]
        counts = [(last - first) * tok for first, last in chunks]
        q_rows = [padded(n) for n in counts]
        o_rows = [padded(n + BLOCK) for n in counts]
        g_rows = width // LANES * tok + 2 * BLOCK
        any_spec = pl.BlockSpec(memory_space=pl.ANY)
        dma = pltpu.SemaphoreType.DMA

        def per_chunk(slots, rows):
            return [pltpu.VMEM((slots, n, LANES), BF16) for n in rows]

        n_chunk = len(chunks)
        return pl.pallas_call(
            functools.partial(kernel, n_head, chunks),
            out_shape=pltpu.VMEM((tok, width), BF16),
            in_specs=[any_spec] * 9,
            out_specs=pl.BlockSpec(memory_space=pltpu.VMEM),
            scratch_shapes=[
                pltpu.SMEM(patch_layout.shape, jnp.int32),
                pltpu.SMEM((tok // BLOCK, 2, heads), jnp.int32),
                pltpu.SMEM((1,), jnp.int32),
                pltpu.VMEM((tok, channels), BF16),
                pltpu.VMEM((tok, channels), BF16),
                pltpu.VMEM((tok, channels), BF16),
                pltpu.VMEM(cache_table.shape[1:], BF16),
                pltpu.VMEM((channels, dout), BF16),
                pltpu.VMEM(gate_table.shape, F32),
                per_chunk(ny, q_rows),
                per_chunk(nxz, [2 * n for n in counts]),
                per_chunk(ny, o_rows),
                per_chunk(ny, o_rows),
                pltpu.VMEM((tok, dout), F32),
                pltpu.VMEM((2 * n_head, g_rows, LANES), BF16),
                pltpu.VMEM((2 * n_head, g_rows, LANES), BF16),
                dma((9,)),
                dma((n_chunk, ny)),
                dma((n_chunk, ny)),
                dma((n_chunk, nxz)),
                dma((n_chunk, nxz)),
                dma((n_chunk, ny)),
                dma((n_chunk, ny)),
                dma((2 * n_head,)),
                dma((2 * n_head,)),
            ],
            compiler_params=pltpu.CompilerParams(
                collective_id=0, has_side_effects=True, vmem_limit_bytes=60 * 2**20
            ),
        )(
            patch_layout,
            jnp.transpose(exponents[0], (1, 0, 2)),
            timestep,
            queries[0],
            keys_new[0],
            values_new[0],
            cache_table[0],
            out_weight,
            gate_table,
        )

    in_specs = (
        P("cfg", "patch", "head"),
        P("cfg", "patch", "head"),
        P("cfg", "patch", "head"),
        P("cfg", None, None, "head"),
        P("cfg", None, "patch", "head"),
        P(),
        P("head", None),
        P(None, ("cfg", "head")),
        P(),
    )
    out_specs = P("patch", ("cfg", "head"))
    return jax.shard_map(local, mesh=mesh, in_specs=in_specs, out_specs=out_specs, check_vma=False)
```

```python
import functools
import math

import jax
import jax.numpy as jnp
from jax import lax
from jax.experimental import pallas as pl
from jax.experimental.pallas import tpu as pltpu
from jax.sharding import PartitionSpec as P

MESH = pl.DeviceIdType.MESH
BLOCK = 8
LANES = 128
GRID = (2, 4, 8)

F32 = jnp.float32
BF16 = jnp.bfloat16


def dot_t(a, b):
    return lax.dot_general(a, b, (((1,), (1,)), ((), ())), preferred_element_type=F32)


def far_first(count):
    return sorted(range(1, count), key=lambda step: -min(step, count - step))


def padded(count):
    return -(-count // 16) * 16


def kernel(
    n_head,
    chunks,
    layout_in,
    exponents_in,
    timestep_in,
    queries,
    keys_new,
    values_new,
    cache_table,
    out_weight,
    gate_table,
    out,
    layout,
    exponents,
    timestep,
    q_in,
    k_in,
    v_in,
    table,
    weight,
    gate,
    q_all,
    kv_all,
    o_send,
    o_recv,
    projected,
    g_send,
    g_recv,
    local_sem,
    q_ssem,
    q_rsem,
    kv_ssem,
    kv_rsem,
    o_ssem,
    o_rsem,
    g_ssem,
    g_rsem,
):
    nz, nx, ny = GRID
    nxz = nz * nx
    tok = q_in.shape[0]
    heads = q_in.shape[1] // LANES
    blocks = tok // BLOCK
    width = out.shape[1]

    cfg = lax.axis_index("cfg")
    patch = lax.axis_index("patch")
    head = lax.axis_index("head")
    y = lax.rem(patch, ny)
    xz = lax.div(patch, ny)
    x = lax.rem(xz, nx)
    z = lax.div(xz, nx)

    def y_partner(step):
        return (cfg, xz * ny + lax.rem(y + step + ny, ny), head)

    def xz_partner(dz, dx):
        other_z = lax.rem(z + dz, nz)
        other_x = lax.rem(x + dx, nx)
        return (cfg, (other_z * nx + other_x) * ny + y, head)

    def feature_partner(swap, step):
        return (1 - cfg if swap else cfg, patch, lax.rem(head + step, n_head))

    def send(src, dst, ssem, rsem, device):
        copy = pltpu.make_async_remote_copy(
            src_ref=src,
            dst_ref=dst,
            send_sem=ssem,
            recv_sem=rsem,
            device_id=device,
            device_id_type=MESH,
        )
        copy.start()
        return copy

    y_steps = far_first(ny)
    xz_steps = [(1, dx) for dx in far_first(nx)] if nz > 1 else []
    xz_steps += [(0, dx) for dx in far_first(nx)]
    xz_steps += [(1, 0)] if nz > 1 else []
    feature_steps = [(swap, s) for s in far_first(n_head) for swap in (1, 0)] + [(1, 0)]

    partners = [y_partner(s) for s in y_steps] + [xz_partner(*s) for s in xz_steps]
    partners += [feature_partner(*s) for s in feature_steps]
    pairs = [
        (queries, q_in),
        (layout_in, layout),
        (exponents_in, exponents),
        (keys_new, k_in),
        (cache_table.at[0], table.at[0]),
        (values_new, v_in),
        (cache_table.at[1], table.at[1]),
        (timestep_in, timestep),
        (gate_table, gate),
        (out_weight, weight),
    ]
    local = [pltpu.make_async_copy(a, b, local_sem.at[i]) for i, (a, b) in enumerate(pairs)]
    for copy in local[:7]:
        copy.start()
    barrier = pltpu.get_barrier_semaphore()
    for partner in partners:
        pl.semaphore_signal(barrier, inc=1, device_id=partner, device_id_type=MESH)

    local[0].wait()
    own_q = q_in[...].astype(F32)
    for c, (first, last) in enumerate(chunks):
        rows = [own_q[:, h * LANES : (h + 1) * LANES] for h in range(first, last)]
        extra = q_all[c].shape[1] - (last - first) * tok
        rows += [jnp.zeros((extra, LANES), F32)] if extra else []
        q_all[c][0] = jnp.concatenate(rows, axis=0).astype(BF16)

    local[1].wait()
    lane = lax.broadcasted_iota(jnp.int32, (BLOCK, table.shape[1]), 1)
    sub = lax.broadcasted_iota(jnp.int32, (BLOCK, table.shape[1]), 0)
    picks = []
    for b in range(blocks):
        wanted = jnp.zeros(lane.shape, jnp.int32)
        for i in range(BLOCK):
            wanted = jnp.where(sub == i, layout[patch * tok + b * BLOCK + i], wanted)
        picks.append(jnp.where(lane == wanted, 1.0, 0.0).astype(F32))
    onehot = jnp.concatenate(picks, axis=0).astype(BF16)

    local[2].wait()
    full = [[], []]
    for kind, fresh_ref in enumerate((k_in, v_in)):
        local[3 + 2 * kind].wait()
        local[4 + 2 * kind].wait()
        cached = jnp.dot(onehot, table[kind], preferred_element_type=F32)
        fresh = fresh_ref[...].astype(F32)
        for h in range(heads):
            for b in range(blocks):
                power = exponents[b, kind, h]
                factor = jnp.where(power == -8, 2.0**-8, jnp.where(power == -7, 2.0**-7, 2.0**-6))
                inverse = jnp.where(power == -8, 2.0**8, jnp.where(power == -7, 2.0**7, 2.0**6))
                where = (slice(b * BLOCK, (b + 1) * BLOCK), slice(h * LANES, (h + 1) * LANES))
                old = cached[where]
                scaled = jnp.clip((fresh[where] - old) * inverse, -448.0, 448.0)
                residual = scaled.astype(BF16).astype(F32) * factor
                full[kind].append(old + residual)
    for c, (first, last) in enumerate(chunks):
        part = slice(first * blocks, last * blocks)
        kv_all[c][0] = jnp.concatenate(full[0][part] + full[1][part], axis=0).astype(BF16)

    pl.semaphore_wait(barrier, len(partners))

    gathers = [[] for _ in chunks]
    for c, q in enumerate(q_all):
        for s in y_steps:
            copy = send(q.at[0], q.at[s], q_ssem.at[c, s], q_rsem.at[c, s], y_partner(s))
            gathers[c].append(copy)
    for c, kv in enumerate(kv_all):
        for dz, dx in xz_steps:
            e = dz * nx + dx
            copy = send(kv.at[0], kv.at[e], kv_ssem.at[c, e], kv_rsem.at[c, e], xz_partner(dz, dx))
            gathers[c].append(copy)
    for copy in local[7:]:
        copy.start()

    inverse_root = 1.0 / math.sqrt(LANES)
    sub8 = lax.broadcasted_iota(jnp.int32, (BLOCK, LANES), 0)

    def diagonal(rows):
        shape = (rows, LANES)
        return lax.broadcasted_iota(jnp.int32, shape, 0) == lax.broadcasted_iota(jnp.int32, shape, 1)

    o_sends = []
    for c, (first, last) in enumerate(chunks):
        for copy in gathers[c]:
            copy.wait_recv()
        rows = (last - first) * tok
        eye = diagonal(rows)
        q_f = [q_all[c][s].astype(F32) for s in range(ny)]
        kv_f = [kv_all[c][e].astype(F32) for e in range(nxz)]
        outs, lses = [], []
        for h in range(last - first):
            k0, v0 = h * tok, rows + h * tok
            q_h = jnp.concatenate([q[k0 : k0 + tok] for q in q_f], axis=0).astype(BF16)
            k_h = jnp.concatenate([kv[k0 : k0 + tok] for kv in kv_f], axis=0).astype(BF16)
            v_h = jnp.concatenate([kv[v0 : v0 + tok] for kv in kv_f], axis=0).astype(BF16)
            scores = dot_t(q_h, k_h) * inverse_root
            top = jnp.max(scores, axis=1, keepdims=True)
            weights = jnp.exp(scores - top)
            total = jnp.sum(weights, axis=1, keepdims=True)
            mixed = jnp.dot(weights.astype(BF16), v_h, preferred_element_type=F32)
            outs.append(mixed / total)
            lses.append(top + jnp.log(total))
        copies = []
        for s in y_steps + [0]:
            part = slice(s * tok, (s + 1) * tok)
            lse = jnp.concatenate([v[part] for v in lses], axis=0)
            lse = jnp.sum(jnp.where(eye, lse, 0.0), axis=0, keepdims=True)
            high = lse.astype(BF16).astype(F32)
            mid = (lse - high).astype(BF16).astype(F32)
            low = lse - high - mid
            stats = jnp.where(sub8 == 0, high, jnp.where(sub8 == 1, mid, jnp.where(sub8 == 2, low, 0.0)))
            extra = o_recv[c].shape[1] - rows - BLOCK
            pad = [jnp.zeros((extra, LANES), F32)] if extra else []
            message = jnp.concatenate([o[part] for o in outs] + [stats] + pad, axis=0).astype(BF16)
            if s == 0:
                o_recv[c][0] = message
            else:
                o_send[c][s] = message
                copies.append(
                    send(o_send[c].at[s], o_recv[c].at[s], o_ssem.at[c, s], o_rsem.at[c, s], y_partner(-s))
                )
        o_sends.append(copies)

    for copy in local[7:]:
        copy.wait()
    for c, (first, last) in enumerate(chunks):
        for copy in o_sends[c]:
            copy.wait_recv()
        rows = (last - first) * tok
        eye = diagonal(rows)
        o_f = [o_recv[c][s].astype(F32) for s in range(ny)]
        lse_rows = []
        for o in o_f:
            lse_rows.append(o[rows : rows + 1] + o[rows + 1 : rows + 2] + o[rows + 2 : rows + 3])
        top = functools.reduce(jnp.maximum, lse_rows)
        shares = [jnp.exp(v - top) for v in lse_rows]
        total = functools.reduce(jnp.add, shares)
        attended = jnp.zeros((rows, LANES), F32)
        for o, share in zip(o_f, shares):
            column = jnp.sum(jnp.where(eye, share / total, 0.0), axis=1, keepdims=True)
            attended = attended + o[:rows] * column
        by_head = [attended[h * tok : (h + 1) * tok] for h in range(last - first)]
        product = jnp.dot(
            jnp.concatenate(by_head, axis=1).astype(BF16),
            weight[first * LANES : last * LANES, :],
            preferred_element_type=F32,
        )
        projected[...] = product if c == 0 else projected[...] + product

    coefficient = jnp.where(cfg == 0, 5.0, -4.0)
    n_full, rest = width // LANES, width % LANES
    lane16 = lax.broadcasted_iota(jnp.int32, (2 * BLOCK, LANES), 1)

    def features(swap, step):
        block = (1 - cfg if swap else cfg) * n_head + lax.rem(head + step, n_head)
        odd = lax.rem(block, 2) == 1
        start = pl.multiple_of(block * width // LANES * LANES, LANES)
        term = projected[:, pl.ds(start, (n_full + 1) * LANES)] * coefficient
        tiles = [term[:, i * LANES : (i + 1) * LANES] for i in range(n_full + 1)]
        half = jnp.where(odd, tiles[0], tiles[-1])
        beside = jnp.concatenate([half[2 * BLOCK :], jnp.zeros((BLOCK, LANES), F32)], axis=0)
        own_lanes = (lane16 >= rest) == odd
        packed = jnp.where(own_lanes, half[: 2 * BLOCK], pltpu.roll(beside, rest, 1))
        pieces = [jnp.where(odd, tiles[i + 1], tiles[i]) for i in range(n_full)]
        return jnp.concatenate(pieces + [packed], axis=0)

    g_sends = []
    for swap, s in feature_steps:
        slot = swap * n_head + s
        g_send[slot] = features(swap, s).astype(BF16)
        g_sends.append(
            send(g_send.at[slot], g_recv.at[slot], g_ssem.at[slot], g_rsem.at[slot], feature_partner(swap, s))
        )
    here = lax.broadcasted_iota(jnp.int32, gate.shape, 0) == timestep[0]
    gate_row = jnp.sum(jnp.where(here, gate[...], 0.0), axis=0, keepdims=True)
    summed = features(0, 0)
    for (swap, s), copy in zip(feature_steps, g_sends):
        copy.wait_recv()
        summed = summed + g_recv[swap * n_head + s].astype(F32)
    whole = [summed[i * tok : (i + 1) * tok] for i in range(n_full)]
    packed = summed[n_full * tok :]
    turned = pltpu.roll(packed, rest, 1)
    low = jnp.concatenate([packed, turned[:BLOCK]], axis=0)[:, :rest]
    high = jnp.concatenate([turned, packed[:BLOCK]], axis=0)[:, :rest]
    total = jnp.where(
        lax.rem(head, 2) == 0,
        jnp.concatenate(whole + [low], axis=1),
        jnp.concatenate([high] + whole, axis=1),
    )
    out[...] = (total * gate_row).astype(out.dtype)

    for copy in sum(gathers + o_sends, []) + g_sends:
        copy.wait_send()


def solution(mesh):
    n_head = mesh.shape["head"]

    def local(
        queries,
        keys_new,
        values_new,
        cache_table,
        exponents,
        patch_layout,
        out_weight,
        gate_table,
        timestep,
    ):
        nz, nx, ny = GRID
        nxz = nz * nx
        _, tok, channels = queries.shape
        heads = channels // LANES
        dout = out_weight.shape[1]
        width = dout // 2 // n_head
        chunks = [(0, heads // 2), (heads // 2, heads)]
        counts = [(last - first) * tok for first, last in chunks]
        q_rows = [padded(n) for n in counts]
        o_rows = [padded(n + BLOCK) for n in counts]
        g_rows = width // LANES * tok + 2 * BLOCK
        any_spec = pl.BlockSpec(memory_space=pl.ANY)
        dma = pltpu.SemaphoreType.DMA

        def per_chunk(slots, rows):
            return [pltpu.VMEM((slots, n, LANES), BF16) for n in rows]

        n_chunk = len(chunks)
        return pl.pallas_call(
            functools.partial(kernel, n_head, chunks),
            out_shape=pltpu.VMEM((tok, width), BF16),
            in_specs=[any_spec] * 9,
            out_specs=pl.BlockSpec(memory_space=pltpu.VMEM),
            scratch_shapes=[
                pltpu.SMEM(patch_layout.shape, jnp.int32),
                pltpu.SMEM((tok // BLOCK, 2, heads), jnp.int32),
                pltpu.SMEM((1,), jnp.int32),
                pltpu.VMEM((tok, channels), BF16),
                pltpu.VMEM((tok, channels), BF16),
                pltpu.VMEM((tok, channels), BF16),
                pltpu.VMEM(cache_table.shape[1:], BF16),
                pltpu.VMEM((channels, dout), BF16),
                pltpu.VMEM(gate_table.shape, F32),
                per_chunk(ny, q_rows),
                per_chunk(nxz, [2 * n for n in counts]),
                per_chunk(ny, o_rows),
                per_chunk(ny, o_rows),
                pltpu.VMEM((tok, dout), F32),
                pltpu.VMEM((2 * n_head, g_rows, LANES), BF16),
                pltpu.VMEM((2 * n_head, g_rows, LANES), BF16),
                dma((10,)),
                dma((n_chunk, ny)),
                dma((n_chunk, ny)),
                dma((n_chunk, nxz)),
                dma((n_chunk, nxz)),
                dma((n_chunk, ny)),
                dma((n_chunk, ny)),
                dma((2 * n_head,)),
                dma((2 * n_head,)),
            ],
            compiler_params=pltpu.CompilerParams(
                collective_id=0, has_side_effects=True, vmem_limit_bytes=60 * 2**20
            ),
        )(
            patch_layout,
            jnp.transpose(exponents[0], (1, 0, 2)),
            timestep,
            queries[0],
            keys_new[0],
            values_new[0],
            cache_table[0],
            out_weight,
            gate_table,
        )

    in_specs = (
        P("cfg", "patch", "head"),
        P("cfg", "patch", "head"),
        P("cfg", "patch", "head"),
        P("cfg", None, None, "head"),
        P("cfg", None, "patch", "head"),
        P(),
        P("head", None),
        P(None, ("cfg", "head")),
        P(),
    )
    out_specs = P("patch", ("cfg", "head"))
    return jax.shard_map(local, mesh=mesh, in_specs=in_specs, out_specs=out_specs, check_vma=False)
```

```python
import functools
import math

import jax
import jax.numpy as jnp
from jax import lax
from jax.experimental import pallas as pl
from jax.experimental.pallas import tpu as pltpu
from jax.sharding import PartitionSpec as P

MESH = pl.DeviceIdType.MESH
BLOCK = 8
LANES = 128
GRID = (2, 4, 8)

F32 = jnp.float32
BF16 = jnp.bfloat16


def dot_t(a, b):
    return lax.dot_general(a, b, (((1,), (1,)), ((), ())), preferred_element_type=F32)


def far_first(count):
    return sorted(range(1, count), key=lambda step: -min(step, count - step))


def padded(count):
    return -(-count // 16) * 16


def kernel(
    n_head,
    chunks,
    layout_in,
    exponents_in,
    timestep_in,
    queries,
    keys_new,
    values_new,
    cache_table,
    out_weight,
    gate_table,
    out,
    layout,
    exponents,
    timestep,
    q_in,
    k_in,
    v_in,
    table,
    weight,
    gate,
    q_all,
    kv_all,
    o_send,
    o_recv,
    projected,
    g_send,
    g_recv,
    local_sem,
    q_ssem,
    q_rsem,
    kv_ssem,
    kv_rsem,
    o_ssem,
    o_rsem,
    g_ssem,
    g_rsem,
):
    nz, nx, ny = GRID
    nxz = nz * nx
    tok = q_in.shape[0]
    heads = q_in.shape[1] // LANES
    blocks = tok // BLOCK
    width = out.shape[1]

    cfg = lax.axis_index("cfg")
    patch = lax.axis_index("patch")
    head = lax.axis_index("head")
    y = lax.rem(patch, ny)
    xz = lax.div(patch, ny)
    x = lax.rem(xz, nx)
    z = lax.div(xz, nx)

    def y_partner(step):
        return (cfg, xz * ny + lax.rem(y + step + ny, ny), head)

    def xz_partner(dz, dx):
        other_z = lax.rem(z + dz, nz)
        other_x = lax.rem(x + dx, nx)
        return (cfg, (other_z * nx + other_x) * ny + y, head)

    def feature_partner(swap, step):
        return (1 - cfg if swap else cfg, patch, lax.rem(head + step, n_head))

    def send(src, dst, ssem, rsem, device):
        copy = pltpu.make_async_remote_copy(
            src_ref=src,
            dst_ref=dst,
            send_sem=ssem,
            recv_sem=rsem,
            device_id=device,
            device_id_type=MESH,
        )
        copy.start()
        return copy

    y_steps = far_first(ny)
    xz_steps = [(1, 2), (0, 2), (1, 1), (1, 3), (0, 1), (0, 3), (1, 0)]
    feature_steps = [(swap, s) for s in far_first(n_head) for swap in (1, 0)] + [(1, 0)]

    partners = [y_partner(s) for s in y_steps] + [xz_partner(*s) for s in xz_steps]
    partners += [feature_partner(*s) for s in feature_steps]
    pairs = [
        (queries, q_in),
        (layout_in, layout),
        (exponents_in, exponents),
        (cache_table, table),
        (keys_new, k_in),
        (values_new, v_in),
        (timestep_in, timestep),
        (gate_table, gate),
        (out_weight, weight),
    ]
    local = [pltpu.make_async_copy(a, b, local_sem.at[i]) for i, (a, b) in enumerate(pairs)]
    for copy in local[:6]:
        copy.start()
    barrier = pltpu.get_barrier_semaphore()
    for partner in partners:
        pl.semaphore_signal(barrier, inc=1, device_id=partner, device_id_type=MESH)

    local[0].wait()
    own_q = q_in[...].astype(F32)
    for c, (first, last) in enumerate(chunks):
        rows = [own_q[:, h * LANES : (h + 1) * LANES] for h in range(first, last)]
        extra = q_all[c].shape[1] - (last - first) * tok
        rows += [jnp.zeros((extra, LANES), F32)] if extra else []
        q_all[c][0] = jnp.concatenate(rows, axis=0).astype(BF16)

    local[1].wait()
    lane = lax.broadcasted_iota(jnp.int32, (BLOCK, table.shape[1]), 1)
    sub = lax.broadcasted_iota(jnp.int32, (BLOCK, table.shape[1]), 0)
    picks = []
    for b in range(blocks):
        wanted = jnp.zeros(lane.shape, jnp.int32)
        for i in range(BLOCK):
            wanted = jnp.where(sub == i, layout[patch * tok + b * BLOCK + i], wanted)
        picks.append(jnp.where(lane == wanted, 1.0, 0.0).astype(F32))
    onehot = jnp.concatenate(picks, axis=0).astype(BF16)

    for copy in local[2:6]:
        copy.wait()
    full = [[], []]
    for kind, fresh_ref in enumerate((k_in, v_in)):
        cached = jnp.dot(onehot, table[kind], preferred_element_type=F32)
        fresh = fresh_ref[...].astype(F32)
        for h in range(heads):
            for b in range(blocks):
                power = exponents[b, kind, h]
                factor = jnp.where(power == -8, 2.0**-8, jnp.where(power == -7, 2.0**-7, 2.0**-6))
                inverse = jnp.where(power == -8, 2.0**8, jnp.where(power == -7, 2.0**7, 2.0**6))
                where = (slice(b * BLOCK, (b + 1) * BLOCK), slice(h * LANES, (h + 1) * LANES))
                old = cached[where]
                scaled = jnp.clip((fresh[where] - old) * inverse, -448.0, 448.0)
                residual = scaled.astype(BF16).astype(F32) * factor
                full[kind].append(old + residual)
    for c, (first, last) in enumerate(chunks):
        part = slice(first * blocks, last * blocks)
        kv_all[c][0] = jnp.concatenate(full[0][part] + full[1][part], axis=0).astype(BF16)

    pl.semaphore_wait(barrier, len(partners))

    gathers = [[] for _ in chunks]
    for c, q in enumerate(q_all):
        for s in y_steps:
            copy = send(q.at[0], q.at[s], q_ssem.at[c, s], q_rsem.at[c, s], y_partner(s))
            gathers[c].append(copy)
    for c, kv in enumerate(kv_all):
        for dz, dx in xz_steps:
            e = dz * nx + dx
            copy = send(kv.at[0], kv.at[e], kv_ssem.at[c, e], kv_rsem.at[c, e], xz_partner(dz, dx))
            gathers[c].append(copy)
    for copy in local[6:]:
        copy.start()

    inverse_root = 1.0 / math.sqrt(LANES)
    sub8 = lax.broadcasted_iota(jnp.int32, (BLOCK, LANES), 0)

    def diagonal(rows):
        shape = (rows, LANES)
        return lax.broadcasted_iota(jnp.int32, shape, 0) == lax.broadcasted_iota(jnp.int32, shape, 1)

    o_sends = []
    for c, (first, last) in enumerate(chunks):
        for copy in gathers[c]:
            copy.wait_recv()
        rows = (last - first) * tok
        eye = diagonal(rows)
        q_f = [q_all[c][s].astype(F32) for s in range(ny)]
        kv_f = [kv_all[c][e].astype(F32) for e in range(nxz)]
        outs, lses = [], []
        for h in range(last - first):
            k0, v0 = h * tok, rows + h * tok
            q_h = jnp.concatenate([q[k0 : k0 + tok] for q in q_f], axis=0).astype(BF16)
            k_h = jnp.concatenate([kv[k0 : k0 + tok] for kv in kv_f], axis=0).astype(BF16)
            v_h = jnp.concatenate([kv[v0 : v0 + tok] for kv in kv_f], axis=0).astype(BF16)
            scores = dot_t(q_h, k_h) * inverse_root
            top = jnp.max(scores, axis=1, keepdims=True)
            weights = jnp.exp(scores - top)
            total = jnp.sum(weights, axis=1, keepdims=True)
            mixed = jnp.dot(weights.astype(BF16), v_h, preferred_element_type=F32)
            outs.append(mixed / total)
            lses.append(top + jnp.log(total))
        copies = []
        for s in y_steps + [0]:
            part = slice(s * tok, (s + 1) * tok)
            lse = jnp.concatenate([v[part] for v in lses], axis=0)
            lse = jnp.sum(jnp.where(eye, lse, 0.0), axis=0, keepdims=True)
            high = lse.astype(BF16).astype(F32)
            mid = (lse - high).astype(BF16).astype(F32)
            low = lse - high - mid
            stats = jnp.where(sub8 == 0, high, jnp.where(sub8 == 1, mid, jnp.where(sub8 == 2, low, 0.0)))
            extra = o_recv[c].shape[1] - rows - BLOCK
            pad = [jnp.zeros((extra, LANES), F32)] if extra else []
            message = jnp.concatenate([o[part] for o in outs] + [stats] + pad, axis=0).astype(BF16)
            if s == 0:
                o_recv[c][0] = message
            else:
                o_send[c][s] = message
                copies.append(
                    send(o_send[c].at[s], o_recv[c].at[s], o_ssem.at[c, s], o_rsem.at[c, s], y_partner(-s))
                )
        o_sends.append(copies)

    for copy in local[6:]:
        copy.wait()
    for c, (first, last) in enumerate(chunks):
        for copy in o_sends[c]:
            copy.wait_recv()
        rows = (last - first) * tok
        eye = diagonal(rows)
        o_f = [o_recv[c][s].astype(F32) for s in range(ny)]
        lse_rows = []
        for o in o_f:
            lse_rows.append(o[rows : rows + 1] + o[rows + 1 : rows + 2] + o[rows + 2 : rows + 3])
        top = functools.reduce(jnp.maximum, lse_rows)
        shares = [jnp.exp(v - top) for v in lse_rows]
        total = functools.reduce(jnp.add, shares)
        attended = jnp.zeros((rows, LANES), F32)
        for o, share in zip(o_f, shares):
            column = jnp.sum(jnp.where(eye, share / total, 0.0), axis=1, keepdims=True)
            attended = attended + o[:rows] * column
        by_head = [attended[h * tok : (h + 1) * tok] for h in range(last - first)]
        product = jnp.dot(
            jnp.concatenate(by_head, axis=1).astype(BF16),
            weight[first * LANES : last * LANES, :],
            preferred_element_type=F32,
        )
        projected[...] = product if c == 0 else projected[...] + product

    coefficient = jnp.where(cfg == 0, 5.0, -4.0)
    n_full, rest = width // LANES, width % LANES
    lane16 = lax.broadcasted_iota(jnp.int32, (2 * BLOCK, LANES), 1)

    def features(swap, step):
        block = (1 - cfg if swap else cfg) * n_head + lax.rem(head + step, n_head)
        odd = lax.rem(block, 2) == 1
        start = pl.multiple_of(block * width // LANES * LANES, LANES)
        term = projected[:, pl.ds(start, (n_full + 1) * LANES)] * coefficient
        tiles = [term[:, i * LANES : (i + 1) * LANES] for i in range(n_full + 1)]
        half = jnp.where(odd, tiles[0], tiles[-1])
        beside = jnp.concatenate([half[2 * BLOCK :], jnp.zeros((BLOCK, LANES), F32)], axis=0)
        own_lanes = (lane16 >= rest) == odd
        packed = jnp.where(own_lanes, half[: 2 * BLOCK], pltpu.roll(beside, rest, 1))
        pieces = [jnp.where(odd, tiles[i + 1], tiles[i]) for i in range(n_full)]
        return jnp.concatenate(pieces + [packed], axis=0)

    g_sends = []
    for swap, s in feature_steps:
        slot = swap * n_head + s
        g_send[slot] = features(swap, s).astype(BF16)
        g_sends.append(
            send(g_send.at[slot], g_recv.at[slot], g_ssem.at[slot], g_rsem.at[slot], feature_partner(swap, s))
        )
    here = lax.broadcasted_iota(jnp.int32, gate.shape, 0) == timestep[0]
    gate_row = jnp.sum(jnp.where(here, gate[...], 0.0), axis=0, keepdims=True)
    summed = features(0, 0)
    for (swap, s), copy in zip(feature_steps, g_sends):
        copy.wait_recv()
        summed = summed + g_recv[swap * n_head + s].astype(F32)
    whole = [summed[i * tok : (i + 1) * tok] for i in range(n_full)]
    packed = summed[n_full * tok :]
    turned = pltpu.roll(packed, rest, 1)
    low = jnp.concatenate([packed, turned[:BLOCK]], axis=0)[:, :rest]
    high = jnp.concatenate([turned, packed[:BLOCK]], axis=0)[:, :rest]
    total = jnp.where(
        lax.rem(head, 2) == 0,
        jnp.concatenate(whole + [low], axis=1),
        jnp.concatenate([high] + whole, axis=1),
    )
    out[...] = (total * gate_row).astype(out.dtype)

    for copy in sum(gathers + o_sends, []) + g_sends:
        copy.wait_send()


def solution(mesh):
    n_head = mesh.shape["head"]

    def local(
        queries,
        keys_new,
        values_new,
        cache_table,
        exponents,
        patch_layout,
        out_weight,
        gate_table,
        timestep,
    ):
        nz, nx, ny = GRID
        nxz = nz * nx
        _, tok, channels = queries.shape
        heads = channels // LANES
        dout = out_weight.shape[1]
        width = dout // 2 // n_head
        chunks = [(0, heads // 2), (heads // 2, heads)]
        counts = [(last - first) * tok for first, last in chunks]
        q_rows = [padded(n) for n in counts]
        o_rows = [padded(n + BLOCK) for n in counts]
        g_rows = width // LANES * tok + 2 * BLOCK
        any_spec = pl.BlockSpec(memory_space=pl.ANY)
        dma = pltpu.SemaphoreType.DMA

        def per_chunk(slots, rows):
            return [pltpu.VMEM((slots, n, LANES), BF16) for n in rows]

        n_chunk = len(chunks)
        return pl.pallas_call(
            functools.partial(kernel, n_head, chunks),
            out_shape=pltpu.VMEM((tok, width), BF16),
            in_specs=[any_spec] * 9,
            out_specs=pl.BlockSpec(memory_space=pltpu.VMEM),
            scratch_shapes=[
                pltpu.SMEM(patch_layout.shape, jnp.int32),
                pltpu.SMEM((tok // BLOCK, 2, heads), jnp.int32),
                pltpu.SMEM((1,), jnp.int32),
                pltpu.VMEM((tok, channels), BF16),
                pltpu.VMEM((tok, channels), BF16),
                pltpu.VMEM((tok, channels), BF16),
                pltpu.VMEM(cache_table.shape[1:], BF16),
                pltpu.VMEM((channels, dout), BF16),
                pltpu.VMEM(gate_table.shape, F32),
                per_chunk(ny, q_rows),
                per_chunk(nxz, [2 * n for n in counts]),
                per_chunk(ny, o_rows),
                per_chunk(ny, o_rows),
                pltpu.VMEM((tok, dout), F32),
                pltpu.VMEM((2 * n_head, g_rows, LANES), BF16),
                pltpu.VMEM((2 * n_head, g_rows, LANES), BF16),
                dma((9,)),
                dma((n_chunk, ny)),
                dma((n_chunk, ny)),
                dma((n_chunk, nxz)),
                dma((n_chunk, nxz)),
                dma((n_chunk, ny)),
                dma((n_chunk, ny)),
                dma((2 * n_head,)),
                dma((2 * n_head,)),
            ],
            compiler_params=pltpu.CompilerParams(
                collective_id=0, has_side_effects=True, vmem_limit_bytes=60 * 2**20
            ),
        )(
            patch_layout,
            jnp.transpose(exponents[0], (1, 0, 2)),
            timestep,
            queries[0],
            keys_new[0],
            values_new[0],
            cache_table[0],
            out_weight,
            gate_table,
        )

    in_specs = (
        P("cfg", "patch", "head"),
        P("cfg", "patch", "head"),
        P("cfg", "patch", "head"),
        P("cfg", None, None, "head"),
        P("cfg", None, "patch", "head"),
        P(),
        P("head", None),
        P(None, ("cfg", "head")),
        P(),
    )
    out_specs = P("patch", ("cfg", "head"))
    return jax.shard_map(local, mesh=mesh, in_specs=in_specs, out_specs=out_specs, check_vma=False)
```
